128 devices in a mesh: tm: 4 (over x_hi, core), height: 4 (over y), head: 8 (over x_lo, z).
Axes of the slice: x: 4 (x_hi: 2, x_lo: 2; x = x_hi * 2 + x_lo), y: 4, z: 4, core: 2. Of those that a mesh axis runs over, the one named last changes fastest.
Arguments:
- query_rows: bfloat16 [16, 4, 4, 768, 128], P('head', 'tm', 'height'), may hold values from -17 to 17
- key_rows: bfloat16 [16, 4, 4, 768, 128], P('head', 'tm', 'height'), may hold values from -17 to 17
- value_rows: bfloat16 [16, 4, 4, 768, 128], P('head', 'tm', 'height'), may hold values from -6 to 6
- out_weight: bfloat16 [2048, 2048], P('head'), may hold values from -0.125 to 0.125
- out_grad: bfloat16 [2048, 4, 4, 768], P('head', 'tm', 'height'), may hold values from -6 to 6
Outputs:
- projected: bfloat16 [2048, 4, 4, 768], P('head', 'tm', 'height')
- query_grad: float32 [16, 4, 4, 768, 128], P('head', 'tm', 'height')
- key_grad: float32 [16, 4, 4, 768, 128], P('head', 'tm', 'height')
- value_grad: float32 [16, 4, 4, 768, 128], P('head', 'tm', 'height')
- weight_grad: float32 [2048, 2048], P('head', ('tm', 'height'))
The draws below stay inside these ranges and needn't reach their ends.
All inputs are finite; a program needn't handle non-finite values.
Results may differ from the reference program's by a relative error of at most 0.025.
Values may be sent and summed in bfloat16 or wider, within the bound.
No kernel may reach another device: no remote copies, remote signals or barrier semaphores. Data moves between devices by JAX's collectives and lax.ppermute only.
A program may use at most 192 MiB of HBM per device.

```python
import math
import jax
import jax.numpy as jnp
from jax import lax

HEADS = 16
HEAD_DIM = 128
D = 2048
TILE = 384
WT = 2
TIME_TILES = 4
ROW_TILES = 4


def drawn_draw(key, low_scale, high_scale):
    full_shape = (HEADS, TIME_TILES, ROW_TILES, WT * TILE, HEAD_DIM)
    row_shape = (HEADS, TIME_TILES, ROW_TILES, WT * TILE, 1)
    entries = jnp.clip(jax.random.normal(jax.random.fold_in(key, 1), full_shape, jnp.float32), -3.5, 3.5)
    logs = jax.random.uniform(jax.random.fold_in(key, 2), row_shape, jnp.float32, math.log(low_scale), math.log(high_scale))
    return entries * jnp.exp(logs)


def draw_query_rows(key, part):
    key = jax.random.fold_in(key, 3)
    drawn = drawn_draw(key, 0.3, 3.0)
    return drawn.astype(jnp.bfloat16)


def draw_key_rows(key, part):
    key = jax.random.fold_in(key, 5)
    drawn = drawn_draw(key, 1.0, 1.25)
    return drawn.astype(jnp.bfloat16)


def shard_levels(rng, extent, split, low, largest):
    loudness, own = 1.0, jax.random.fold_in(rng, 6)
    for dim, shards_of in split:
        steps = jnp.exp(jax.random.uniform(jax.random.fold_in(own, dim), (shards_of,), jnp.float32, low / len(split), largest / len(split)))
        loudness = loudness * jnp.repeat(steps, extent[dim] // shards_of).reshape([-1 if axis == dim else 1 for axis in range(len(extent))])
    return loudness


def noise(own_key, dims, deviation, most, pieces=(), kind=jnp.bfloat16):
    level = shard_levels(own_key, dims, pieces, -0.22, 0.18) if pieces else 1.0
    values = jax.random.normal(own_key, dims, jnp.float32) * deviation * level
    return jnp.minimum(jnp.maximum(values, -most), most).astype(kind)


def setup_inputs(seed: int = 0) -> dict:
    key_list = jax.random.split(jax.random.key(seed), 6)
    query_rows = draw_query_rows(jax.random.fold_in(key_list[5], 71), 0)
    key_rows = draw_key_rows(jax.random.fold_in(key_list[5], 71), 0)
    value_rows = noise(key_list[2], (HEADS, TIME_TILES, ROW_TILES, WT * TILE, HEAD_DIM), 1.0, 6.0, ((0, 8), (1, 4), (2, 4)))
    out_weight = noise(key_list[3], (D, D), D ** -0.5, 0.125, ((0, 8),))
    out_grad = noise(key_list[4], (D, TIME_TILES, ROW_TILES, WT * TILE), 1.0, 6.0, ((0, 8), (1, 4), (2, 4)))
    return {"query_rows": query_rows, "key_rows": key_rows, "value_rows": value_rows, "out_weight": out_weight, "out_grad": out_grad}


def as_tiles(source):
    shaped = source.reshape((HEADS, TIME_TILES, ROW_TILES, WT, TILE) + source.shape[4:])
    padding = ((0, 0), (1, 1), (1, 1), (0, 0), (0, 0)) + ((0, 0),) * (source.ndim - 4)
    return jnp.pad(shaped, padding)

def window_of(padded, time_tile, row_tile, width_start, width_span):
    anchor = time_tile * 0
    offsets = (anchor, time_tile, row_tile, width_start, anchor) + (anchor,) * (padded.ndim - 5)
    window = lax.dynamic_slice(padded, offsets, (HEADS, 3, 3, width_span, TILE) + padded.shape[5:])
    return window.reshape((HEADS, 9 * width_span * TILE) + padded.shape[5:])

def own_tile(padded, time_tile, row_tile, width_tile):
    anchor = time_tile * 0
    offsets = (anchor, time_tile + 1, row_tile + 1, width_tile, anchor) + (anchor,) * (padded.ndim - 5)
    window = lax.dynamic_slice(padded, offsets, (HEADS, 1, 1, 1, TILE) + padded.shape[5:])
    return window.reshape((HEADS, TILE) + padded.shape[5:])

def visible_keys(time_tile, row_tile, width_tile, width_start, width_span):
    nearby = jnp.arange(3, dtype=jnp.int32) - 1
    time_visible = (time_tile + nearby >= 0) & (time_tile + nearby < TIME_TILES)
    row_visible = (row_tile + nearby >= 0) & (row_tile + nearby < ROW_TILES)
    across = jnp.arange(width_span, dtype=jnp.int32) + width_start
    width_visible = jnp.abs(across - width_tile) <= 1
    allowed = time_visible[:, None, None] & row_visible[None, :, None] & width_visible[None, None, :]
    return jnp.repeat(allowed.reshape(-1), TILE)

def split_id(tile_id):
    time_tile = tile_id // (ROW_TILES * WT)
    row_tile = tile_id // WT % ROW_TILES
    width_tile = tile_id % WT
    return (time_tile, row_tile, width_tile)

def start_of(width_tile, width_span):
    return jnp.clip(width_tile - 1, 0, WT - width_span).astype(jnp.int32)

def from_tiles(stacked):
    shaped = stacked.reshape((TIME_TILES, ROW_TILES, WT, HEADS, TILE) + stacked.shape[3:])
    moved = jnp.moveaxis(shaped, 3, 0)
    return moved.reshape((HEADS, TIME_TILES, ROW_TILES, WT * TILE) + stacked.shape[3:])

def reference(query_rows, key_rows, value_rows, out_weight, out_grad):
    width_span = min(3, WT)
    factor = 1.0 / math.sqrt(HEAD_DIM)
    query_pad = as_tiles(query_rows)
    key_pad = as_tiles(key_rows)
    value_pad = as_tiles(value_rows)
    tile_ids = jnp.arange(TIME_TILES * ROW_TILES * WT, dtype=jnp.int32)

    def tile_scores(tile_id):
        time_tile, row_tile, width_tile = split_id(tile_id)
        width_start = start_of(width_tile, width_span)
        query_tile = own_tile(query_pad, time_tile, row_tile, width_tile).astype(jnp.float32)
        key_window = window_of(key_pad, time_tile, row_tile, width_start, width_span).astype(jnp.float32)
        value_window = window_of(value_pad, time_tile, row_tile, width_start, width_span).astype(jnp.float32)
        allowed = visible_keys(time_tile, row_tile, width_tile, width_start, width_span)
        scores = jnp.einsum('hqd,hkd->hqk', query_tile, key_window) * factor
        scores = jnp.where(allowed[None, None, :], scores, -jnp.inf)
        return (query_tile, key_window, value_window, scores)

    def forward_tile(tile_id):
        query_tile, key_window, value_window, scores = tile_scores(tile_id)
        row_max = lax.optimization_barrier(jnp.max(scores, -1, keepdims=True))
        log_total = row_max[..., 0] + jnp.log(lax.optimization_barrier(jnp.sum(jnp.exp(scores - row_max), -1)))
        weights = jnp.exp(scores - log_total[..., None])
        rounded = lax.optimization_barrier(weights.astype(jnp.bfloat16)).astype(jnp.float32)
        attended = jnp.einsum('hqk,hkd->hqd', rounded, value_window).astype(jnp.bfloat16)
        return (attended, log_total)
    attended_tiles, log_tiles = lax.map(forward_tile, tile_ids)
    attended = from_tiles(attended_tiles)
    log_total = from_tiles(log_tiles)
    token_count = TIME_TILES * ROW_TILES * WT * TILE
    attended_flat = jnp.transpose(attended, (0, 4, 1, 2, 3)).reshape(D, token_count)
    projected = jnp.dot(out_weight.T, attended_flat, preferred_element_type=jnp.float32)
    projected = projected.astype(jnp.bfloat16).reshape(D, TIME_TILES, ROW_TILES, WT * TILE)
    grad_flat = out_grad.reshape(D, token_count)
    attn_flat = jnp.dot(out_weight, grad_flat, preferred_element_type=jnp.float32).astype(jnp.bfloat16)
    attn_grad = jnp.transpose(attn_flat.reshape(HEADS, HEAD_DIM, TIME_TILES, ROW_TILES, WT * TILE), (0, 2, 3, 4, 1))
    weight_grad = jnp.dot(attended_flat, grad_flat.T, preferred_element_type=jnp.float32)
    row_dot = lax.optimization_barrier(jnp.sum(attn_grad.astype(jnp.float32) * attended.astype(jnp.float32), -1))
    attn_pad = as_tiles(attn_grad)
    log_pad = as_tiles(log_total)
    dot_pad = as_tiles(row_dot)

    def add_window(total, part, time_tile, row_tile, width_start):
        anchor = time_tile * 0
        offsets = (anchor, time_tile, row_tile, width_start, anchor, anchor)
        paired = part.reshape(HEADS, 3, 3, width_span, TILE, HEAD_DIM)
        current = lax.dynamic_slice(total, offsets, paired.shape)
        return lax.dynamic_update_slice(total, current + paired, offsets)

    def backward_tile(totals, tile_id):
        key_total, value_total = totals
        time_tile, row_tile, width_tile = split_id(tile_id)
        width_start = start_of(width_tile, width_span)
        query_tile, key_window, value_window, scores = tile_scores(tile_id)
        log_tile = own_tile(log_pad, time_tile, row_tile, width_tile)
        dot_tile = own_tile(dot_pad, time_tile, row_tile, width_tile)
        grad_tile = own_tile(attn_pad, time_tile, row_tile, width_tile).astype(jnp.float32)
        weights = jnp.exp(scores - log_tile[..., None])
        rounded = lax.optimization_barrier(weights.astype(jnp.bfloat16)).astype(jnp.float32)
        prob_grad = jnp.einsum('hqe,hke->hqk', grad_tile, value_window)
        score_grad = weights * (prob_grad - dot_tile[..., None])
        score_grad = lax.optimization_barrier(score_grad.astype(jnp.bfloat16)).astype(jnp.float32)
        query_part = jnp.einsum('hqk,hke->hqe', score_grad, key_window) * factor
        key_part = jnp.einsum('hqk,hqe->hke', score_grad, query_tile) * factor
        value_part = jnp.einsum('hqk,hqe->hke', rounded, grad_tile)
        key_total = add_window(key_total, key_part, time_tile, row_tile, width_start)
        value_total = add_window(value_total, value_part, time_tile, row_tile, width_start)
        return ((key_total, value_total), query_part)
    empty = jnp.zeros(key_pad.shape, jnp.float32)
    (key_total, value_total), query_parts = lax.scan(backward_tile, (empty, empty), tile_ids)
    query_grad = from_tiles(query_parts)
    full_shape = (HEADS, TIME_TILES, ROW_TILES, WT * TILE, HEAD_DIM)
    key_grad = key_total[:, 1:-1, 1:-1].reshape(full_shape)
    value_grad = value_total[:, 1:-1, 1:-1].reshape(full_shape)
    return (projected, query_grad, key_grad, value_grad, weight_grad)
```

```python
import functools
import math

import jax
import jax.numpy as jnp
from jax import lax
from jax.experimental import pallas as pl
from jax.experimental.pallas import tpu as pltpu
from jax.sharding import PartitionSpec as P

FORWARD_CHUNK = 256
BACKWARD_CHUNK = 256
VMEM = pl.BlockSpec(memory_space=pltpu.VMEM)
SMEM = pl.BlockSpec(memory_space=pltpu.SMEM)
HBM = pl.BlockSpec(memory_space=pltpu.HBM)
COST = pl.CostEstimate(flops=1000000, bytes_accessed=1000, transcendentals=0)
NT = (((1,), (1,)), ((), ()))
NN = (((1,), (0,)), ((), ()))
FORWARD_LIMIT = 24 * 1024 * 1024
BACKWARD_LIMIT = 28 * 1024 * 1024


def mm(a, b, dims=NN):
    return lax.dot_general(a, b, dims, preferred_element_type=jnp.float32)


def forward_kernel(ids, first, last, scale, *refs):
    count = len(ids)
    valid, queries = refs[:2]
    pairs = refs[2 : 2 + count]
    rest = refs[2 + count :]
    if not first:
        max_in, sum_in, acc_in = rest[:3]
        rest = rest[3:]
    prob_out = rest[:count]
    ref_out, max_now, sum_now, acc_now = rest[count : count + 4]
    rest = rest[count + 4 :]
    if last:
        attended, rest = (rest[0], rest[1:])
    scores_0, scores_1, probs, sems = rest
    scores = (scores_0, scores_1)
    heads, tokens, depth = queries.shape
    if first:
        max_now[...] = jnp.full(max_now.shape, -1e30, jnp.float32)
        sum_now[...] = jnp.zeros(sum_now.shape, jnp.float32)
        acc_now[...] = jnp.zeros(acc_now.shape, jnp.float32)
    else:
        max_now[...] = max_in[...]
        sum_now[...] = sum_in[...]
        acc_now[...] = acc_in[...]
    chains = [(h, c) for h in range(heads) for c in range(0, tokens, FORWARD_CHUNK)]

    def copy_out(index):
        return pltpu.make_async_copy(probs.at[index % 2], prob_out[index], sems.at[index % 2])

    for index in range(count):
        slot = index % 2
        if index >= 2:
            copy_out(index - 2).wait()

        @pl.when(valid[ids[index]] > 0)
        def _():
            pair = pairs[index]
            values = []
            for h in range(heads):
                ones = jnp.ones((16, tokens), jnp.bfloat16)
                values.append(jnp.concatenate([pair[1, h].T, ones], axis=0))

            def score(place):
                h, c = chains[place]
                s = mm(pair[0, h], queries[h, c : c + FORWARD_CHUNK, :], NT)
                scores[place % 2][...] = s
                return jnp.max(s, axis=0, keepdims=True) * scale

            block_max = score(0)
            for place, (h, c) in enumerate(chains):
                cols = slice(c, c + FORWARD_CHUNK)
                if place + 1 < len(chains):
                    later = score(place + 1)
                before = max_now[h, :, cols]
                now = jnp.maximum(before, block_max)
                p = jnp.exp2(scores[place % 2][...] * scale - now).astype(jnp.bfloat16)
                probs[slot, h, :, cols] = p
                part = mm(values[h], p)
                fade = jnp.exp2(before - now)
                max_now[h, :, cols] = now
                ref_out[index, h, :, cols] = now
                acc_now[h, :, cols] = acc_now[h, :, cols] * fade + part[:depth]
                sum_now[h, :, cols] = sum_now[h, :, cols] * fade + part[depth : depth + 1]
                block_max = later

        copy_out(index).start()
    for index in range(max(0, count - 2), count):
        copy_out(index).wait()
    if last:
        for h in range(heads):
            attended[h] = (acc_now[h] / sum_now[h]).astype(jnp.bfloat16)


def forward_call(ids, valid, queries, pairs, state, last, scale):
    count = len(ids)
    heads, tokens, depth = queries.shape
    f32 = jnp.float32
    row = jax.ShapeDtypeStruct((heads, 1, tokens), f32)
    outs = [pltpu.HBM((heads, tokens, tokens), jnp.bfloat16)] * count
    outs += [jax.ShapeDtypeStruct((count, heads, 1, tokens), f32), row, row]
    outs += [jax.ShapeDtypeStruct((heads, depth, tokens), f32)]
    if last:
        outs += [jax.ShapeDtypeStruct((heads, depth, tokens), jnp.bfloat16)]
    first = state is None
    operands = [valid, queries, *pairs] + ([] if first else list(state))
    results = pl.pallas_call(
        functools.partial(forward_kernel, ids, first, last, scale),
        out_shape=outs,
        in_specs=[SMEM] + [VMEM] * (len(operands) - 1),
        out_specs=[HBM] * count + [VMEM] * (len(outs) - count),
        scratch_shapes=[
            pltpu.VMEM((tokens, FORWARD_CHUNK), f32),
            pltpu.VMEM((tokens, FORWARD_CHUNK), f32),
            pltpu.VMEM((2, heads, tokens, tokens), jnp.bfloat16),
            pltpu.SemaphoreType.DMA((2,)),
        ],
        compiler_params=pltpu.CompilerParams(vmem_limit_bytes=FORWARD_LIMIT),
        cost_estimate=COST,
        name="forward" + str(count),
    )(*operands)
    return (
        results[:count],
        results[count],
        results[count + 1 : count + 4],
        results[count + 4 :],
    )


def backward_kernel(ids, groups, adds, first, last, factor, *refs):
    count = len(ids)
    valid, queries, grads, attended = refs[:4]
    tops = refs[4 : 4 + len(groups)]
    top, total = refs[4 + len(groups) : 6 + len(groups)]
    rest = refs[6 + len(groups) :]
    pairs, prob_in, rest = (rest[:count], rest[count : 2 * count], rest[2 * count :])
    if not first:
        query_in, rest = (rest[0], rest[1:])
    added = []
    for terms in adds:
        added.append(rest[: len(terms)])
        rest = rest[len(terms) :]
    part_out = rest[:count]
    query_out, acc, probs, grads_0, grads_1, sems = rest[count:]
    score_grads = (grads_0, grads_1)
    heads, tokens, depth = queries.shape
    where = {i: (g, place) for g, ids_in in enumerate(groups) for place, i in enumerate(ids_in)}

    def copy_in(index):
        return pltpu.make_async_copy(prob_in[index], probs.at[index % 2], sems.at[index % 2])

    for index in range(min(2, count)):
        copy_in(index).start()
    if first:
        acc[...] = jnp.zeros(acc.shape, jnp.float32)
    else:
        acc[...] = query_in[...]
    dots = [
        jnp.sum(
            grads[h].astype(jnp.float32) * attended[h].astype(jnp.float32), axis=0, keepdims=True
        )
        for h in range(heads)
    ]
    chains = [(h, c) for h in range(heads) for c in range(0, tokens, BACKWARD_CHUNK)]
    for index in range(count):
        slot = index % 2
        copy_in(index).wait()

        @pl.when(valid[ids[index]] > 0)
        def _():
            pair, out = (pairs[index], part_out[index])
            group, place_in = where[ids[index]]
            grad, dot, turned = ([], [], [])
            for h in range(heads):
                keep = jnp.exp2(tops[group][place_in, h] - top[h]) / total[h]
                grad.append((grads[h].astype(jnp.float32) * keep).astype(jnp.bfloat16))
                dot.append(dots[h] * keep)
                turned.append(pair[0, h].T)

            def prob_grad(h, c):
                return mm(pair[1, h], grad[h][:, c : c + BACKWARD_CHUNK])

            def finish(kind, h, value):
                for ref, at in zip(added[index], adds[index]):
                    extra = ref[kind, h] if at is None else ref[at, kind, h]
                    value = value + extra.astype(jnp.float32)
                out[kind, h] = value.astype(out.dtype)

            now = prob_grad(*chains[0])
            for place, (h, c) in enumerate(chains):
                cols = slice(c, c + BACKWARD_CHUNK)
                if place + 1 < len(chains):
                    later = prob_grad(*chains[place + 1])
                if c == 0:
                    finish(1, h, mm(probs[slot, h], grad[h], NT))
                weights = probs[slot, h, :, cols].astype(jnp.float32)
                ds = (weights * (now - dot[h][:, cols])).astype(jnp.bfloat16)
                score_grads[h][:, cols] = ds
                acc[h, :, cols] += mm(turned[h], ds)
                if c + BACKWARD_CHUNK == tokens:
                    finish(0, h, mm(score_grads[h][...], queries[h]) * factor)
                now = later

        if index + 2 < count:
            copy_in(index + 2).start()
    if last:
        for h in range(heads):
            query_out[h] = acc[h].T * factor
    else:
        query_out[...] = acc[...]


def backward_call(ids, groups, valid, queries, grads, attended, tops, state, pairs, probs, query, added, kinds, last, factor):
    count = len(ids)
    heads, tokens, depth = queries.shape
    f32 = jnp.float32
    first = query is None
    outs = [jax.ShapeDtypeStruct((2, heads, tokens, depth), kind) for kind in kinds]
    query_shape = (heads, tokens, depth) if last else (heads, depth, tokens)
    outs += [jax.ShapeDtypeStruct(query_shape, f32)]
    probs = [pltpu.with_memory_space_constraint(p, pltpu.HBM) for p in probs]
    operands = [valid, queries, grads, attended, *tops, *state, *pairs, *probs]
    specs = [SMEM] + [VMEM] * (len(operands) - 1 - count) + [HBM] * count
    more = ([] if first else [query]) + [term for terms in added for term, _ in terms]
    adds = tuple(tuple(at for _, at in terms) for terms in added)
    results = pl.pallas_call(
        functools.partial(backward_kernel, ids, groups, adds, first, last, factor),
        out_shape=outs,
        in_specs=specs + [VMEM] * len(more),
        out_specs=[VMEM] * len(outs),
        scratch_shapes=[
            pltpu.VMEM((heads, depth, tokens), f32),
            pltpu.VMEM((2, heads, tokens, tokens), jnp.bfloat16),
            pltpu.VMEM((tokens, tokens), jnp.bfloat16),
            pltpu.VMEM((tokens, tokens), jnp.bfloat16),
            pltpu.SemaphoreType.DMA((2,)),
        ],
        compiler_params=pltpu.CompilerParams(vmem_limit_bytes=BACKWARD_LIMIT),
        cost_estimate=COST,
        name="backward" + str(count),
    )(*operands, *more)
    return (results[:count], results[count])


def shards(query_rows, key_rows, value_rows, out_weight, out_grad):
    heads, _, _, tokens, depth = query_rows.shape
    factor = 1.0 / math.sqrt(depth)
    scale = factor * math.log2(math.e)
    times, rows = (lax.axis_size("tm"), lax.axis_size("height"))
    both = ("tm", "height")

    def grid(pairs):
        return [(a * rows + b, a2 * rows + b2) for (a, b), (a2, b2) in pairs]

    every = [(a, b) for a in range(times) for b in range(rows)]
    crossing = [a for a in range(times) if 0 <= (a - 1 if a % 2 == 0 else a + 1) < times]

    def across(a):
        return a - 1 if a % 2 == 0 else a + 1

    up = grid([((a, b), (a, b + 1)) for a, b in every if b + 1 < rows])
    down = grid([((a, b), (a, b - 1)) for a, b in every if b >= 1])
    partner = grid([((a, b), (a ^ 1, b)) for a, b in every])
    cross = grid([((a, b), (across(a), b)) for a, b in every if a in crossing])
    cross_up = grid([((a, b), (a, b + 1)) for a, b in every if a in crossing and b + 1 < rows])
    cross_down = grid([((a, b), (a, b - 1)) for a, b in every if a in crossing and b >= 1])

    def send(value, route):
        return lax.ppermute(value, both, route)

    time, row = (lax.axis_index("tm"), lax.axis_index("height"))
    other = jnp.where(time % 2 == 0, time - 1, time + 1)
    crossed = (other >= 0) & (other < times)
    above, below = (row > 0, row < rows - 1)
    yes = row >= 0
    valid = jnp.stack(
        [yes, above, below, yes, above, below, crossed, crossed & above, crossed & below]
    ).astype(jnp.int32)

    queries = query_rows[:, 0, 0]
    own = jnp.stack((key_rows[:, 0, 0], value_rows[:, 0, 0]))
    out_share = out_grad.shape[0]
    grad_flat = out_grad.reshape(out_share, tokens)
    half = lax.axis_size("head") // 2
    side = lax.axis_index("head") // half
    rings = [list(range(half)), list(range(half, 2 * half))]
    swapped = lax.ppermute(
        grad_flat, "head", [(i, (i + half) % (2 * half)) for i in range(2 * half)]
    )

    def around(value):
        return lax.all_gather(value, "head", axis_index_groups=rings, axis=0, tiled=True)

    grad_here, grad_there = (around(grad_flat), around(swapped))
    width = half * out_share
    weight_here = lax.dynamic_slice_in_dim(out_weight, side * width, width, 1)
    weight_there = lax.dynamic_slice_in_dim(out_weight, (1 - side) * width, width, 1)
    grads = mm(weight_here, grad_here) + mm(weight_there, grad_there)
    grads = grads.astype(jnp.bfloat16).reshape(heads, depth, tokens)

    slabs, probs, refs = ([None] * 9, [None] * 9, [])
    groups = ((0, 3), (1, 2, 6), (4, 5, 7, 8))

    def forward(ids, state):
        got, ref, state, extra = forward_call(
            ids, valid, queries, [slabs[i] for i in ids], state, ids is groups[-1], scale
        )
        refs.append(ref)
        for place, i in enumerate(ids):
            probs[i] = got[place]
        return (state, extra)

    slabs[0] = own
    slabs[6] = send(own, cross)
    slabs[1] = send(own, up)
    slabs[2] = send(own, down)
    slabs[3] = send(own, partner)
    state, _ = forward(groups[0], None)
    slabs[6], *state = lax.optimization_barrier((slabs[6], *state))
    slabs[7] = send(slabs[6], cross_up)
    slabs[8] = send(slabs[6], cross_down)
    slabs[4] = send(slabs[1], partner)
    slabs[5] = send(slabs[2], partner)
    state, _ = forward(groups[1], state)
    state, extra = forward(groups[2], state)
    attended = extra[0]
    attended_flat = attended.reshape(heads * depth, tokens)

    projected = mm(out_weight.T, attended_flat).astype(jnp.bfloat16)
    projected = lax.psum_scatter(projected, "head", scatter_dimension=0, tiled=True)
    projected = projected.reshape(out_share, 1, 1, tokens)
    part_here = mm(attended_flat, grad_here, NT).astype(jnp.bfloat16)
    part_there = mm(attended_flat, grad_there, NT).astype(jnp.bfloat16)
    weight_part = jnp.stack(
        [jnp.where(side == 0, part_here, part_there), jnp.where(side == 0, part_there, part_here)]
    )
    shares = times * rows
    weight_part = weight_part.reshape(2, heads * depth, shares // 2, -1).transpose(0, 2, 1, 3)
    weight_part = weight_part.reshape(shares, heads * depth, -1)
    weight_terms = lax.all_to_all(weight_part, both, 0, 0)
    weight_grad = jnp.sum(weight_terms.astype(jnp.float32), axis=0)

    total = state[:2]

    def backward(ids, query, added=None, last=False):
        kinds = [jnp.float32 if i == 0 else jnp.bfloat16 for i in ids]
        added = added or [()] * len(ids)
        return backward_call(
            ids, groups, valid, queries, grads, attended, refs, total,
            [slabs[i] for i in ids], [probs[i] for i in ids], query, added, kinds, last, factor,
        )

    def add(*terms):
        whole = terms[0].astype(jnp.float32)
        for term in terms[1:]:
            whole = whole + term.astype(jnp.float32)
        return whole

    (part_7, part_8), query = backward((7, 8), None)
    back_up = send(part_7, cross_down)
    back_down = send(part_8, cross_up)
    (part_4, part_5), query = backward((4, 5), query)
    near_up = send(part_4, partner)
    near_down = send(part_5, partner)
    (part_6, part_3), query = backward((6, 3), query, [((back_up, None), (back_down, None)), ()])
    far = send(part_6, cross)
    near = send(part_3, partner)
    (part_1, part_2), query = backward((1, 2), query, [((near_up, None),), ((near_down, None),)])
    to_up = send(part_1, down)
    to_down = send(part_2, up)
    (part_0,), query_grad = backward((0,), query, [((near, None),)], True)
    owned = [add(part_0[k], far[k], to_up[k], to_down[k]) for k in (0, 1)]
    grad_shape = (heads, 1, 1, tokens, depth)
    return (
        projected,
        query_grad.reshape(grad_shape),
        owned[0].reshape(grad_shape),
        owned[1].reshape(grad_shape),
        weight_grad,
    )


def solution(mesh):
    rows = P("head", "tm", "height", None, None)
    columns = P("head", "tm", "height", None)
    return jax.shard_map(
        shards,
        mesh=mesh,
        in_specs=(rows, rows, rows, P("head", None), columns),
        out_specs=(columns, rows, rows, rows, P("head", ("tm", "height"))),
        check_vma=False,
    )
```

```python
import functools
import math

import jax
import jax.numpy as jnp
from jax import lax
from jax.experimental import pallas as pl
from jax.experimental.pallas import tpu as pltpu
from jax.sharding import PartitionSpec as P

FORWARD_CHUNK = 256
BACKWARD_CHUNK = 256
VMEM = pl.BlockSpec(memory_space=pltpu.VMEM)
SMEM = pl.BlockSpec(memory_space=pltpu.SMEM)
COST = pl.CostEstimate(flops=1000000, bytes_accessed=1000, transcendentals=0)
LOWEST = -1e30
NT = (((1,), (1,)), ((), ()))
NN = (((1,), (0,)), ((), ()))
FORWARD_LIMIT = 14 * 1024 * 1024
BACKWARD_LIMIT = 14 * 1024 * 1024


def mm(a, b, dims=NN):
    return lax.dot_general(a, b, dims, preferred_element_type=jnp.float32)


def forward_kernel(ids, first, last, scale, *refs):
    count = len(ids)
    valid, queries = refs[:2]
    pairs = refs[2 : 2 + count]
    rest = refs[2 + count :]
    if not first:
        max_in, sum_in, acc_in = rest[:3]
        rest = rest[3:]
    prob_out = rest[:count]
    ref_out, max_now, sum_now, acc_now = rest[count : count + 4]
    rest = rest[count + 4 :]
    if last:
        attended, rest = (rest[0], rest[1:])
    scores = rest
    heads, tokens, depth = queries.shape
    if first:
        max_now[...] = jnp.full(max_now.shape, LOWEST, jnp.float32)
        sum_now[...] = jnp.zeros(sum_now.shape, jnp.float32)
        acc_now[...] = jnp.zeros(acc_now.shape, jnp.float32)
    else:
        max_now[...] = max_in[...]
        sum_now[...] = sum_in[...]
        acc_now[...] = acc_in[...]
    chains = [
        (index, h, c)
        for index in range(count)
        for h in range(heads)
        for c in range(0, tokens, FORWARD_CHUNK)
    ]
    ones = jnp.ones((16, tokens), jnp.bfloat16)
    values = {}

    def score(place):
        index, h, c = chains[place]
        if c == 0:
            values[index, h] = jnp.concatenate([pairs[index][1, h].T, ones], axis=0)
        s = mm(pairs[index][0, h], queries[h, c : c + FORWARD_CHUNK, :], NT)
        scores[place % 2][...] = s
        return jnp.max(s, axis=0, keepdims=True) * scale

    block_max = score(0)
    for place, (index, h, c) in enumerate(chains):
        cols = slice(c, c + FORWARD_CHUNK)
        if place + 1 < len(chains):
            later = score(place + 1)
        seen = valid[ids[index]] > 0
        before = max_now[h, :, cols]
        now = jnp.where(seen, jnp.maximum(before, block_max), before)
        level = jnp.where(seen, now, -LOWEST)
        p = jnp.exp2(scores[place % 2][...] * scale - level).astype(jnp.bfloat16)
        prob_out[index][h, :, cols] = p
        part = mm(values[index, h], p)
        fade = jnp.exp2(before - now)
        max_now[h, :, cols] = now
        ref_out[index, h, :, cols] = now
        acc_now[h, :, cols] = acc_now[h, :, cols] * fade + part[:depth]
        sum_now[h, :, cols] = sum_now[h, :, cols] * fade + part[depth : depth + 1]
        block_max = later
    if last:
        for h in range(heads):
            attended[h] = (acc_now[h] / sum_now[h]).astype(jnp.bfloat16)


def forward_call(ids, valid, queries, pairs, state, last, scale):
    count = len(ids)
    heads, tokens, depth = queries.shape
    f32 = jnp.float32
    row = jax.ShapeDtypeStruct((heads, 1, tokens), f32)
    outs = [pltpu.VMEM((heads, tokens, tokens), jnp.bfloat16)] * count
    outs += [jax.ShapeDtypeStruct((count, heads, 1, tokens), f32), row, row]
    outs += [jax.ShapeDtypeStruct((heads, depth, tokens), f32)]
    if last:
        outs += [jax.ShapeDtypeStruct((heads, depth, tokens), jnp.bfloat16)]
    first = state is None
    operands = [valid, queries, *pairs] + ([] if first else list(state))
    results = pl.pallas_call(
        functools.partial(forward_kernel, ids, first, last, scale),
        out_shape=outs,
        in_specs=[SMEM] + [VMEM] * (len(operands) - 1),
        out_specs=[VMEM] * len(outs),
        scratch_shapes=[pltpu.VMEM((tokens, FORWARD_CHUNK), f32)] * 2,
        compiler_params=pltpu.CompilerParams(vmem_limit_bytes=FORWARD_LIMIT),
        cost_estimate=COST,
        name="forward" + str(count),
    )(*operands)
    return (
        results[:count],
        results[count],
        results[count + 1 : count + 4],
        results[count + 4 :],
    )


def backward_kernel(ids, groups, adds, first, last, factor, *refs):
    count = len(ids)
    queries, grads, attended = refs[:3]
    tops = refs[3 : 3 + len(groups)]
    top, total = refs[3 + len(groups) : 5 + len(groups)]
    rest = refs[5 + len(groups) :]
    pairs, probs, rest = (rest[:count], rest[count : 2 * count], rest[2 * count :])
    if not first:
        query_in, rest = (rest[0], rest[1:])
    added = []
    for terms in adds:
        added.append(rest[: len(terms)])
        rest = rest[len(terms) :]
    part_out = rest[:count]
    query_out, acc, *score_grads = rest[count:]
    heads, tokens, depth = queries.shape
    where = {i: (g, place) for g, ids_in in enumerate(groups) for place, i in enumerate(ids_in)}
    if first:
        acc[...] = jnp.zeros(acc.shape, jnp.float32)
    else:
        acc[...] = query_in[...]
    dots = [
        jnp.sum(
            grads[h].astype(jnp.float32) * attended[h].astype(jnp.float32), axis=0, keepdims=True
        )
        for h in range(heads)
    ]
    chains = [
        (index, h, c)
        for index in range(count)
        for h in range(heads)
        for c in range(0, tokens, BACKWARD_CHUNK)
    ]
    grad, dot, turned = ({}, {}, {})

    def prob_grad(index, h, c):
        if c == 0:
            group, place_in = where[ids[index]]
            keep = jnp.exp2(tops[group][place_in, h] - top[h]) / total[h]
            grad[index, h] = (grads[h].astype(jnp.float32) * keep).astype(jnp.bfloat16)
            dot[index, h] = dots[h] * keep
            turned[index, h] = pairs[index][0, h].T
        return mm(pairs[index][1, h], grad[index, h][:, c : c + BACKWARD_CHUNK])

    def finish(index, kind, h, value):
        for ref, at in zip(added[index], adds[index]):
            extra = ref[kind, h] if at is None else ref[at, kind, h]
            value = value + extra.astype(jnp.float32)
        part_out[index][kind, h] = value.astype(part_out[index].dtype)

    now = prob_grad(*chains[0])
    for place, (index, h, c) in enumerate(chains):
        cols = slice(c, c + BACKWARD_CHUNK)
        if place + 1 < len(chains):
            later = prob_grad(*chains[place + 1])
        if c == 0:
            finish(index, 1, h, mm(probs[index][h], grad[index, h], NT))
        weights = probs[index][h, :, cols].astype(jnp.float32)
        ds = (weights * (now - dot[index, h][:, cols])).astype(jnp.bfloat16)
        held = score_grads[(index * heads + h) % len(score_grads)]
        held[:, cols] = ds
        acc[h, :, cols] += mm(turned[index, h], ds)
        if c + BACKWARD_CHUNK == tokens:
            finish(index, 0, h, mm(held[...], queries[h]) * factor)
        now = later
    if last:
        for h in range(heads):
            query_out[h] = acc[h].T * factor
    else:
        query_out[...] = acc[...]


def backward_call(ids, groups, queries, grads, attended, tops, state, pairs, probs, query, added, kinds, last, factor):
    count = len(ids)
    heads, tokens, depth = queries.shape
    f32 = jnp.float32
    first = query is None
    outs = [jax.ShapeDtypeStruct((2, heads, tokens, depth), kind) for kind in kinds]
    query_shape = (heads, tokens, depth) if last else (heads, depth, tokens)
    outs += [jax.ShapeDtypeStruct(query_shape, f32)]
    probs = [pltpu.with_memory_space_constraint(p, pltpu.VMEM) for p in probs]
    operands = [queries, grads, attended, *tops, *state, *pairs, *probs]
    operands += [] if first else [query]
    operands += [term for terms in added for term, _ in terms]
    adds = tuple(tuple(at for _, at in terms) for terms in added)
    results = pl.pallas_call(
        functools.partial(backward_kernel, ids, groups, adds, first, last, factor),
        out_shape=outs,
        in_specs=[VMEM] * len(operands),
        out_specs=[VMEM] * len(outs),
        scratch_shapes=[
            pltpu.VMEM((heads, depth, tokens), f32),
            pltpu.VMEM((tokens, tokens), jnp.bfloat16),
            pltpu.VMEM((tokens, tokens), jnp.bfloat16),
        ],
        compiler_params=pltpu.CompilerParams(vmem_limit_bytes=BACKWARD_LIMIT),
        cost_estimate=COST,
        name="backward" + str(count),
    )(*operands)
    return (results[:count], results[count])


def shards(query_rows, key_rows, value_rows, out_weight, out_grad):
    heads, _, _, tokens, depth = query_rows.shape
    factor = 1.0 / math.sqrt(depth)
    scale = factor * math.log2(math.e)
    times, rows = (lax.axis_size("tm"), lax.axis_size("height"))
    both = ("tm", "height")

    def grid(pairs):
        return [(a * rows + b, a2 * rows + b2) for (a, b), (a2, b2) in pairs]

    every = [(a, b) for a in range(times) for b in range(rows)]
    crossing = [a for a in range(times) if 0 <= (a - 1 if a % 2 == 0 else a + 1) < times]

    def across(a):
        return a - 1 if a % 2 == 0 else a + 1

    up = grid([((a, b), (a, b + 1)) for a, b in every if b + 1 < rows])
    down = grid([((a, b), (a, b - 1)) for a, b in every if b >= 1])
    partner = grid([((a, b), (a ^ 1, b)) for a, b in every])
    cross = grid([((a, b), (across(a), b)) for a, b in every if a in crossing])
    cross_up = grid([((a, b), (a, b + 1)) for a, b in every if a in crossing and b + 1 < rows])
    cross_down = grid([((a, b), (a, b - 1)) for a, b in every if a in crossing and b >= 1])

    def send(value, route):
        return lax.ppermute(value, both, route)

    time, row = (lax.axis_index("tm"), lax.axis_index("height"))
    other = jnp.where(time % 2 == 0, time - 1, time + 1)
    crossed = (other >= 0) & (other < times)
    above, below = (row > 0, row < rows - 1)
    yes = row >= 0
    valid = jnp.stack(
        [yes, above, below, yes, above, below, crossed, crossed & above, crossed & below]
    ).astype(jnp.int32)

    queries = query_rows[:, 0, 0]
    own = jnp.stack((key_rows[:, 0, 0], value_rows[:, 0, 0]))
    out_share = out_grad.shape[0]
    grad_flat = out_grad.reshape(out_share, tokens)
    slabs, probs, refs = ([None] * 9, [None] * 9, [])
    groups = ((0, 3), (1, 2, 6), (4, 5, 7, 8))

    def forward(ids, state):
        got, ref, state, extra = forward_call(
            ids, valid, queries, [slabs[i] for i in ids], state, ids is groups[-1], scale
        )
        refs.append(ref)
        for place, i in enumerate(ids):
            probs[i] = got[place]
        return (state, extra)

    slabs[0] = own
    slabs[6] = send(own, cross)
    slabs[1] = send(own, up)
    slabs[2] = send(own, down)
    slabs[3] = send(own, partner)
    state, _ = forward(groups[0], None)
    grad_later, *state = lax.optimization_barrier((grad_flat, *state))
    slabs[6], *state = lax.optimization_barrier((slabs[6], *state))

    half = lax.axis_size("head") // 2
    side = lax.axis_index("head") // half
    rings = [list(range(half)), list(range(half, 2 * half))]
    swapped = lax.ppermute(
        grad_later, "head", [(i, (i + half) % (2 * half)) for i in range(2 * half)]
    )

    def around(value):
        return lax.all_gather(value, "head", axis_index_groups=rings, axis=0, tiled=True)

    grad_here, grad_there = (around(grad_flat), around(swapped))
    width = half * out_share
    weight_here = lax.dynamic_slice_in_dim(out_weight, side * width, width, 1)
    weight_there = lax.dynamic_slice_in_dim(out_weight, (1 - side) * width, width, 1)
    grads = mm(weight_here, grad_here) + mm(weight_there, grad_there)
    grads = grads.astype(jnp.bfloat16).reshape(heads, depth, tokens)

    slabs[7] = send(slabs[6], cross_up)
    slabs[8] = send(slabs[6], cross_down)
    slabs[4] = send(slabs[1], partner)
    slabs[5] = send(slabs[2], partner)
    state, _ = forward(groups[1], state)
    state, extra = forward(groups[2], state)
    attended = extra[0]
    attended_flat = attended.reshape(heads * depth, tokens)

    projected = mm(out_weight.T, attended_flat).astype(jnp.bfloat16)
    projected = lax.psum_scatter(projected, "head", scatter_dimension=0, tiled=True)
    projected = projected.reshape(out_share, 1, 1, tokens)
    part_here = mm(attended_flat, grad_here, NT).astype(jnp.bfloat16)
    part_there = mm(attended_flat, grad_there, NT).astype(jnp.bfloat16)
    weight_part = jnp.stack(
        [jnp.where(side == 0, part_here, part_there), jnp.where(side == 0, part_there, part_here)]
    )
    shares = times * rows
    weight_part = weight_part.reshape(2, heads * depth, shares // 2, -1).transpose(0, 2, 1, 3)
    weight_part = weight_part.reshape(shares, heads * depth, -1)
    weight_terms = lax.all_to_all(weight_part, both, 0, 0)
    weight_grad = jnp.sum(weight_terms.astype(jnp.float32), axis=0)

    total = state[:2]

    def backward(ids, query, added=None, last=False):
        kinds = [jnp.float32 if i == 0 else jnp.bfloat16 for i in ids]
        added = added or [()] * len(ids)
        return backward_call(
            ids, groups, queries, grads, attended, refs, total,
            [slabs[i] for i in ids], [probs[i] for i in ids], query, added, kinds, last, factor,
        )

    def add(*terms):
        whole = terms[0].astype(jnp.float32)
        for term in terms[1:]:
            whole = whole + term.astype(jnp.float32)
        return whole

    (part_7, part_8), query = backward((7, 8), None)
    back_up = send(part_7, cross_down)
    back_down = send(part_8, cross_up)
    (part_4, part_5), query = backward((4, 5), query)
    near_up = send(part_4, partner)
    near_down = send(part_5, partner)
    (part_6, part_3), query = backward((6, 3), query, [((back_up, None), (back_down, None)), ()])
    far = send(part_6, cross)
    near = send(part_3, partner)
    (part_1, part_2), query = backward((1, 2), query, [((near_up, None),), ((near_down, None),)])
    to_up = send(part_1, down)
    to_down = send(part_2, up)
    (part_0,), query_grad = backward((0,), query, [((near, None),)], True)
    owned = [add(part_0[k], far[k], to_up[k], to_down[k]) for k in (0, 1)]
    grad_shape = (heads, 1, 1, tokens, depth)
    return (
        projected,
        query_grad.reshape(grad_shape),
        owned[0].reshape(grad_shape),
        owned[1].reshape(grad_shape),
        weight_grad,
    )


def solution(mesh):
    rows = P("head", "tm", "height", None, None)
    columns = P("head", "tm", "height", None)
    return jax.shard_map(
        shards,
        mesh=mesh,
        in_specs=(rows, rows, rows, P("head", None), columns),
        out_specs=(columns, rows, rows, rows, P("head", ("tm", "height"))),
        check_vma=False,
    )
```

```python
import functools
import math

import jax
import jax.numpy as jnp
from jax import lax
from jax.experimental import pallas as pl
from jax.experimental.pallas import tpu as pltpu
from jax.sharding import PartitionSpec as P

FORWARD_CHUNK = 256
BACKWARD_CHUNK = 256
VMEM = pl.BlockSpec(memory_space=pltpu.VMEM)
HBM = pl.BlockSpec(memory_space=pltpu.HBM)
SMEM = pl.BlockSpec(memory_space=pltpu.SMEM)
FORWARD_COST = pl.CostEstimate(flops=30 * 10**9, bytes_accessed=1000, transcendentals=0)
BACKWARD_COST = pl.CostEstimate(flops=1000000, bytes_accessed=1000, transcendentals=0)
LOWEST = -1e30
NT = (((1,), (1,)), ((), ()))
NN = (((1,), (0,)), ((), ()))
TN = (((0,), (0,)), ((), ()))
FORWARD_LIMIT = 24 * 1024 * 1024
BACKWARD_LIMIT = 34 * 1024 * 1024


def mm(a, b, dims=NN):
    return lax.dot_general(a, b, dims, preferred_element_type=jnp.float32)


def forward_kernel(ids, seen, last, scale, *refs):
    count = len(ids)
    valid, queries = refs[:2]
    pairs = refs[2 : 2 + count]
    rest = refs[2 + count :]
    if seen:
        levels_in, max_in, sum_in, acc_in = rest[:4]
        rest = rest[4:]
    if last:
        weight, rest = (rest[0], rest[1:])
    prob_out = rest[:count]
    levels, max_now, sum_now, acc_now = rest[count : count + 4]
    rest = rest[count + 4 :]
    if last:
        attended, projected, rest = (rest[0], rest[1], rest[2:])
    scores, probs, sems = (rest[:2], rest[2], rest[3])
    heads, tokens, depth = queries.shape
    if seen:
        levels[:seen] = levels_in[...]
        max_now[...] = max_in[...]
        sum_now[...] = sum_in[...]
        acc_now[...] = acc_in[...]
    else:
        max_now[...] = jnp.full(max_now.shape, LOWEST, jnp.float32)
        sum_now[...] = jnp.zeros(sum_now.shape, jnp.float32)
        acc_now[...] = jnp.zeros(acc_now.shape, jnp.float32)
    chains = [(h, c) for h in range(heads) for c in range(0, tokens, FORWARD_CHUNK)]

    def copy_out(index):
        return pltpu.make_async_copy(probs.at[index % 2], prob_out[index], sems.at[index % 2])

    for index in range(count):
        slot = index % 2
        if index >= 2:
            copy_out(index - 2).wait()

        @pl.when(valid[ids[index]] > 0)
        def _():
            pair = pairs[index]
            ones = jnp.ones((16, tokens), jnp.bfloat16)
            values = [jnp.concatenate([pair[1, h].T, ones], axis=0) for h in range(heads)]

            def score(place):
                h, c = chains[place]
                s = mm(pair[0, h], queries[h, c : c + FORWARD_CHUNK, :], NT)
                scores[place % 2][...] = s
                return jnp.max(s, axis=0, keepdims=True) * scale

            block_max = score(0)
            for place, (h, c) in enumerate(chains):
                cols = slice(c, c + FORWARD_CHUNK)
                if place + 1 < len(chains):
                    later = score(place + 1)
                before = max_now[h, :, cols]
                now = jnp.maximum(before, block_max)
                p = jnp.exp2(scores[place % 2][...] * scale - now).astype(jnp.bfloat16)
                probs[slot, h, :, cols] = p
                part = mm(values[h], p)
                fade = jnp.exp2(before - now)
                max_now[h, :, cols] = now
                acc_now[h, :, cols] = acc_now[h, :, cols] * fade + part[:depth]
                sum_now[h, :, cols] = sum_now[h, :, cols] * fade + part[depth : depth + 1]
                block_max = later

        @pl.when(valid[ids[index]] == 0)
        def _():
            probs[slot] = jnp.zeros(probs.shape[1:], jnp.bfloat16)

        levels[seen + index] = max_now[...]
        copy_out(index).start()
    if last:
        log_two = math.log2(math.e)
        levels[seen + count] = max_now[...] + jnp.log(sum_now[...]) * log_two
        for h in range(heads):
            rows = slice(h * depth, (h + 1) * depth)
            attended[rows, :] = (acc_now[h] / sum_now[h]).astype(jnp.bfloat16)
        step = heads * depth
        half = projected.shape[0] // (2 * step)
        for place in range(2 * half):
            at = (place % 2) * half + place // 2
            part = mm(weight[:, at * step : (at + 1) * step], attended[...], TN)
            projected[place * step : (place + 1) * step, :] = part.astype(jnp.bfloat16)
    for index in range(max(0, count - 2), count):
        copy_out(index).wait()


def forward_call(ids, seen, valid, queries, pairs, state, weight, scale):
    count = len(ids)
    heads, tokens, depth = queries.shape
    f32, b16 = (jnp.float32, jnp.bfloat16)
    last = weight is not None
    row = jax.ShapeDtypeStruct((heads, 1, tokens), f32)
    outs = [pltpu.HBM((heads, tokens, tokens), b16)] * count
    levels_kind = pltpu.HBM if last else jax.ShapeDtypeStruct
    outs += [levels_kind((seen + count + last, heads, 1, tokens), f32), row, row]
    outs += [jax.ShapeDtypeStruct((heads, depth, tokens), f32)]
    operands = [valid, queries, *pairs] + (list(state) if seen else [])
    if last:
        operands += [weight]
        outs += [jax.ShapeDtypeStruct((heads * depth, tokens), b16)]
        outs += [pltpu.HBM((weight.shape[1], tokens), b16)]
    results = pl.pallas_call(
        functools.partial(forward_kernel, ids, seen, last, scale),
        out_shape=outs,
        in_specs=[SMEM] + [VMEM] * (len(operands) - 1),
        out_specs=[HBM] * count + [VMEM] * (len(outs) - count),
        scratch_shapes=[
            pltpu.VMEM((tokens, FORWARD_CHUNK), f32),
            pltpu.VMEM((tokens, FORWARD_CHUNK), f32),
            pltpu.VMEM((2, heads, tokens, tokens), b16),
            pltpu.SemaphoreType.DMA((2,)),
        ],
        compiler_params=pltpu.CompilerParams(vmem_limit_bytes=FORWARD_LIMIT),
        cost_estimate=FORWARD_COST,
        name="forward" + str(count),
    )(*operands)
    return (results[:count], results[count : count + 4], results[count + 4 :])


def middle_kernel(half, weight, gathered, attended, grads, terms):
    share = gathered.shape[0] // (2 * half)
    each = share // terms.shape[1]
    total = jnp.zeros(grads.shape, jnp.float32)
    for z in range(half):
        for x in range(2):
            block = gathered[(z * 2 + x) * share : (z * 2 + x + 1) * share, :]
            at = x * half + z
            total = total + mm(weight[:, at * share : (at + 1) * share], block)
            term = mm(block, attended[...], NT).astype(jnp.bfloat16)
            for e in range(each):
                terms[at * each + e] = term[e * terms.shape[1] : (e + 1) * terms.shape[1], :]
    grads[...] = total.astype(jnp.bfloat16)


def middle_call(half, shares, weight, gathered, attended):
    b16 = jnp.bfloat16
    rows, columns = weight.shape
    return pl.pallas_call(
        functools.partial(middle_kernel, half),
        out_shape=[
            jax.ShapeDtypeStruct(attended.shape, b16),
            pltpu.HBM((shares, columns // shares, rows), b16),
        ],
        in_specs=[VMEM] * 3,
        out_specs=[VMEM] * 2,
        compiler_params=pltpu.CompilerParams(vmem_limit_bytes=FORWARD_LIMIT),
        cost_estimate=BACKWARD_COST,
        name="middle",
    )(weight, pltpu.with_memory_space_constraint(gathered, pltpu.HBM), attended)


def backward_kernel(outputs, order, adds, extras, first, last, factor, *refs):
    ids = [i for group in outputs for i in group]
    count = len(ids)
    queries, grads, attended, levels = refs[:4]
    rest = refs[4:]
    pairs, prob_in, rest = (rest[:count], rest[count : 2 * count], rest[2 * count :])
    if not first:
        query_in, rest = (rest[0], rest[1:])
    added, rest = (rest[:extras], rest[extras:])
    outs, rest = (rest[: len(outputs)], rest[len(outputs) :])
    part_out = []
    for out, group in zip(outs, outputs):
        part_out += [out] if len(group) == 1 else [out.at[place] for place in range(len(group))]
    query_out, acc, grads_0, grads_1, probs, sems = rest
    score_grads = (grads_0, grads_1)
    heads, tokens, depth = queries.shape

    def copy_in(index, h):
        return pltpu.make_async_copy(prob_in[index].at[h], probs.at[index, h], sems.at[index, h])

    for index in range(count):
        for h in range(heads):
            copy_in(index, h).start()
    if first:
        acc[...] = jnp.zeros(acc.shape, jnp.float32)
    else:
        acc[...] = query_in[...]
    chains = [
        (index, h, c)
        for index in range(count)
        for h in range(heads)
        for c in range(0, tokens, BACKWARD_CHUNK)
    ]
    loads = [(index, h) for index in range(count) for h in range(heads)]
    waits = {(0, 0): loads[:1], (0, 1): loads[1:4], (2, 0): loads[4:]}
    rows = [slice(h * depth, (h + 1) * depth) for h in range(heads)]
    dots = []
    for h in range(heads):
        product = grads[rows[h], :].astype(jnp.float32) * attended[rows[h], :].astype(jnp.float32)
        dots.append(jnp.sum(product, axis=0, keepdims=True))
    grad, dot, turned = ({}, {}, {})

    def prob_grad(index, h, c):
        if c == 0:
            keep = jnp.exp2(levels[order[ids[index]], h] - levels[levels.shape[0] - 1, h])
            grad[index, h] = (grads[rows[h], :].astype(jnp.float32) * keep).astype(jnp.bfloat16)
            dot[index, h] = dots[h] * keep
            turned[index, h] = pairs[index][0, h].T
        return mm(pairs[index][1, h], grad[index, h][:, c : c + BACKWARD_CHUNK])

    def finish(index, kind, h, value):
        for which, at in adds[index]:
            ref = added[which]
            extra = ref[kind, h] if at is None else ref[at, kind, h]
            value = value + extra.astype(jnp.float32)
        part_out[index][kind, h] = value.astype(part_out[index].dtype)

    now = prob_grad(*chains[0])
    for place, (index, h, c) in enumerate(chains):
        cols = slice(c, c + BACKWARD_CHUNK)
        if place + 1 < len(chains):
            later = prob_grad(*chains[place + 1])
        if c == 0:
            for load in waits.get((index, h), ()):
                copy_in(*load).wait()
            finish(index, 1, h, mm(probs[index, h], grad[index, h], NT))
        weights = probs[index, h, :, cols].astype(jnp.float32)
        ds = (weights * (now - dot[index, h][:, cols])).astype(jnp.bfloat16)
        held = score_grads[(index * heads + h) % len(score_grads)]
        held[:, cols] = ds
        acc[h, :, cols] += mm(turned[index, h], ds)
        if c + BACKWARD_CHUNK == tokens:
            finish(index, 0, h, mm(held[...], queries[h]) * factor)
        now = later
    if last:
        for h in range(heads):
            query_out[h] = acc[h].T * factor
    else:
        query_out[...] = acc[...]


def backward_call(outputs, order, queries, grads, attended, levels, slabs, probs, query, added, last, factor):
    ids = [i for group in outputs for i in group]
    count = len(ids)
    heads, tokens, depth = queries.shape
    f32, b16 = (jnp.float32, jnp.bfloat16)
    first = query is None
    outs = []
    for group in outputs:
        several = () if len(group) == 1 else (len(group),)
        kind = jax.ShapeDtypeStruct if last else pltpu.HBM
        outs.append(kind(several + (2, heads, tokens, depth), f32 if last else b16))
    query_shape = (heads, tokens, depth) if last else (heads, depth, tokens)
    outs += [pltpu.HBM(query_shape, f32)]

    def in_hbm(value):
        return pltpu.with_memory_space_constraint(value, pltpu.HBM)

    operands = [queries, grads, attended, in_hbm(levels)]
    operands += [in_hbm(slabs[i]) if i == 0 else slabs[i] for i in ids]
    specs = [VMEM] * len(operands) + [HBM] * count
    operands += [in_hbm(probs[i]) for i in ids]
    operands += [] if first else [in_hbm(query)]
    arrays = []
    adds = []
    for terms in added:
        for term, _ in terms:
            if not any(term is array for array in arrays):
                arrays.append(term)
        which = [next(k for k, array in enumerate(arrays) if term is array) for term, _ in terms]
        adds.append(tuple((k, at) for k, (_, at) in zip(which, terms)))
    operands += arrays
    results = pl.pallas_call(
        functools.partial(backward_kernel, outputs, order, tuple(adds), len(arrays), first, last, factor),
        out_shape=outs,
        in_specs=specs + [VMEM] * (len(operands) - len(specs)),
        out_specs=[VMEM] * len(outs),
        scratch_shapes=[
            pltpu.VMEM((heads, depth, tokens), f32),
            pltpu.VMEM((tokens, tokens), b16),
            pltpu.VMEM((tokens, tokens), b16),
            pltpu.VMEM((count, heads, tokens, tokens), b16),
            pltpu.SemaphoreType.DMA((count, heads)),
        ],
        compiler_params=pltpu.CompilerParams(vmem_limit_bytes=BACKWARD_LIMIT),
        cost_estimate=BACKWARD_COST,
        name="backward" + str(count),
    )(*operands)
    return results


def sum_kernel(*refs):
    terms, outs = (refs[:-2], refs[-2:])
    for kind, out in enumerate(outs):
        whole = terms[0][kind]
        for term in terms[1:]:
            whole = whole + term[kind].astype(jnp.float32)
        out[...] = whole


def sum_call(*terms):
    shape = jax.ShapeDtypeStruct(terms[0].shape[1:], jnp.float32)
    return pl.pallas_call(
        sum_kernel,
        out_shape=[shape, shape],
        in_specs=[VMEM] * len(terms),
        out_specs=[VMEM, VMEM],
        compiler_params=pltpu.CompilerParams(vmem_limit_bytes=FORWARD_LIMIT),
        cost_estimate=BACKWARD_COST,
        name="sums",
    )(*terms)


def shards(query_rows, key_rows, value_rows, out_weight, out_grad):
    heads, _, _, tokens, depth = query_rows.shape
    factor = 1.0 / math.sqrt(depth)
    scale = factor * math.log2(math.e)
    times, rows = (lax.axis_size("tm"), lax.axis_size("height"))
    both = ("tm", "height")

    def grid(pairs):
        return [(a * rows + b, a2 * rows + b2) for (a, b), (a2, b2) in pairs]

    every = [(a, b) for a in range(times) for b in range(rows)]
    crossing = [a for a in range(times) if 0 <= (a - 1 if a % 2 == 0 else a + 1) < times]

    def across(a):
        return a - 1 if a % 2 == 0 else a + 1

    up = grid([((a, b), (a, b + 1)) for a, b in every if b + 1 < rows])
    down = grid([((a, b), (a, b - 1)) for a, b in every if b >= 1])
    partner = grid([((a, b), (a ^ 1, b)) for a, b in every])
    cross = grid([((a, b), (across(a), b)) for a, b in every if a in crossing])
    cross_up = grid([((a, b), (a, b + 1)) for a, b in every if a in crossing and b + 1 < rows])
    cross_down = grid([((a, b), (a, b - 1)) for a, b in every if a in crossing and b >= 1])

    def send(value, route):
        return lax.ppermute(value, both, route)

    time, row = (lax.axis_index("tm"), lax.axis_index("height"))
    other = jnp.where(time % 2 == 0, time - 1, time + 1)
    crossed = (other >= 0) & (other < times)
    above, below = (row > 0, row < rows - 1)
    yes = row >= 0
    valid = jnp.stack(
        [yes, above, below, yes, above, below, crossed, crossed & above, crossed & below]
    ).astype(jnp.int32)

    queries = query_rows[:, 0, 0]
    own = jnp.stack((key_rows[:, 0, 0], value_rows[:, 0, 0]))
    out_share = out_grad.shape[0]
    grad_flat = out_grad.reshape(out_share, tokens)
    half = lax.axis_size("head") // 2
    side = lax.axis_index("head") // half
    rings = [list(range(half)), list(range(half, 2 * half))]
    swap = [(i, (i + half) % (2 * half)) for i in range(2 * half)]
    swapped = lax.ppermute(grad_flat, "head", swap)
    blocks = jnp.where(
        side == 0, jnp.stack([grad_flat, swapped]), jnp.stack([swapped, grad_flat])
    ).reshape(2 * out_share, tokens)
    grad_all = lax.all_gather(blocks, "head", axis_index_groups=rings, axis=0, tiled=True)

    slabs, probs = ([None] * 9, [None] * 9)
    groups = ((0, 3), (1, 2, 6), (4, 5, 7, 8))
    order = {i: place for place, i in enumerate([i for ids in groups for i in ids])}

    def forward(ids, state):
        weight = out_weight if ids is groups[-1] else None
        got, state, extra = forward_call(
            ids, order[ids[0]], valid, queries, [slabs[i] for i in ids], state, weight, scale
        )
        for place, i in enumerate(ids):
            probs[i] = got[place]
        return (state, extra)

    slabs[0] = own
    slabs[6] = send(own, cross)
    slabs[1] = send(own, up)
    slabs[2] = send(own, down)
    slabs[3] = send(own, partner)
    state, _ = forward(groups[0], None)
    slabs[6], *state = lax.optimization_barrier((slabs[6], *state))

    slabs[7] = send(slabs[6], cross_up)
    slabs[8] = send(slabs[6], cross_down)
    slabs[4] = send(slabs[1], partner)
    slabs[5] = send(slabs[2], partner)
    state, _ = forward(groups[1], state)
    state, extra = forward(groups[2], state)
    attended, projected = extra
    levels = state[0]
    projected = lax.psum_scatter(
        projected, "head", scatter_dimension=0, axis_index_groups=rings, tiled=True
    )
    kept = lax.dynamic_slice_in_dim(projected, side * out_share, out_share, 0)
    given = lax.dynamic_slice_in_dim(projected, (1 - side) * out_share, out_share, 0)
    got = lax.ppermute(given, "head", swap)
    projected = (kept.astype(jnp.float32) + got.astype(jnp.float32)).astype(jnp.bfloat16)
    projected = projected.reshape(out_share, 1, 1, tokens)
    grads, weight_part = middle_call(half, times * rows, out_weight, grad_all, attended)
    weight_terms = lax.all_to_all(weight_part, both, 0, 0)
    weight_grad = jnp.sum(weight_terms.astype(jnp.float32), axis=0).T

    def backward(outputs, query, added, last=False):
        return backward_call(
            outputs, order, queries, grads, attended, levels, slabs, probs, query, added, last, factor
        )

    part_7, part_8, part_near, part_3, query = backward(((7,), (8,), (4, 5), (3,)), None, [()] * 5)
    back_up = send(part_7, cross_down)
    back_down = send(part_8, cross_up)
    near = send(part_near, partner)
    near_own = send(part_3, partner)
    weight_grad, query = lax.optimization_barrier((weight_grad, query))
    part_6, part_1, part_2, query = backward(
        ((6,), (1,), (2,)), query, [((back_up, None), (back_down, None)), ((near, 0),), ((near, 1),)]
    )
    far = send(part_6, cross)
    to_up = send(part_1, down)
    to_down = send(part_2, up)
    projected, query = lax.optimization_barrier((projected, query))
    part_0, query_grad = backward(((0,),), query, [((near_own, None),)], True)
    owned = sum_call(part_0, far, to_up, to_down)
    grad_shape = (heads, 1, 1, tokens, depth)
    return (
        projected,
        query_grad.reshape(grad_shape),
        owned[0].reshape(grad_shape),
        owned[1].reshape(grad_shape),
        weight_grad,
    )


def solution(mesh):
    rows = P("head", "tm", "height", None, None)
    columns = P("head", "tm", "height", None)
    return jax.shard_map(
        shards,
        mesh=mesh,
        in_specs=(rows, rows, rows, P("head", None), columns),
        out_specs=(columns, rows, rows, rows, P("head", ("tm", "height"))),
        check_vma=False,
    )
```

```python
import functools
import math

import jax
import jax.numpy as jnp
from jax import lax
from jax.experimental import pallas as pl
from jax.experimental.pallas import tpu as pltpu
from jax.sharding import PartitionSpec as P

FORWARD_CHUNK = 256
BACKWARD_CHUNK = 256
VMEM = pl.BlockSpec(memory_space=pltpu.VMEM)
HBM = pl.BlockSpec(memory_space=pltpu.HBM)
SMEM = pl.BlockSpec(memory_space=pltpu.SMEM)
FORWARD_COST = pl.CostEstimate(flops=30 * 10**9, bytes_accessed=1000, transcendentals=0)
BACKWARD_COST = pl.CostEstimate(flops=1000000, bytes_accessed=1000, transcendentals=0)
LOWEST = -1e30
NT = (((1,), (1,)), ((), ()))
NN = (((1,), (0,)), ((), ()))
TN = (((0,), (0,)), ((), ()))
FORWARD_LIMIT = 24 * 1024 * 1024
BACKWARD_LIMIT = 34 * 1024 * 1024


def mm(a, b, dims=NN):
    return lax.dot_general(a, b, dims, preferred_element_type=jnp.float32)


def forward_kernel(ids, seen, last, scale, *refs):
    count = len(ids)
    valid, queries = refs[:2]
    pairs = refs[2 : 2 + count]
    rest = refs[2 + count :]
    if seen:
        levels_in, max_in, sum_in, acc_in = rest[:4]
        rest = rest[4:]
    if last:
        weight, rest = (rest[0], rest[1:])
    prob_out = rest[:count]
    levels, max_now, sum_now, acc_now = rest[count : count + 4]
    rest = rest[count + 4 :]
    if last:
        attended, projected, rest = (rest[0], rest[1], rest[2:])
    scores, probs, sems = (rest[:2], rest[2], rest[3])
    heads, tokens, depth = queries.shape
    if seen:
        levels[:seen] = levels_in[...]
        max_now[...] = max_in[...]
        sum_now[...] = sum_in[...]
        acc_now[...] = acc_in[...]
    else:
        max_now[...] = jnp.full(max_now.shape, LOWEST, jnp.float32)
        sum_now[...] = jnp.zeros(sum_now.shape, jnp.float32)
        acc_now[...] = jnp.zeros(acc_now.shape, jnp.float32)
    chains = [(h, c) for h in range(heads) for c in range(0, tokens, FORWARD_CHUNK)]

    def copy_out(index):
        return pltpu.make_async_copy(probs.at[index % 2], prob_out[index], sems.at[index % 2])

    for index in range(count):
        slot = index % 2
        if index >= 2:
            copy_out(index - 2).wait()

        @pl.when(valid[ids[index]] > 0)
        def _():
            pair = pairs[index]
            ones = jnp.ones((16, tokens), jnp.bfloat16)
            values = [jnp.concatenate([pair[1, h].T, ones], axis=0) for h in range(heads)]

            def score(place):
                h, c = chains[place]
                s = mm(pair[0, h], queries[h, c : c + FORWARD_CHUNK, :], NT)
                scores[place % 2][...] = s
                return jnp.max(s, axis=0, keepdims=True) * scale

            block_max = score(0)
            for place, (h, c) in enumerate(chains):
                cols = slice(c, c + FORWARD_CHUNK)
                if place + 1 < len(chains):
                    later = score(place + 1)
                before = max_now[h, :, cols]
                now = jnp.maximum(before, block_max)
                p = jnp.exp2(scores[place % 2][...] * scale - now).astype(jnp.bfloat16)
                probs[slot, h, :, cols] = p
                part = mm(values[h], p)
                fade = jnp.exp2(before - now)
                max_now[h, :, cols] = now
                acc_now[h, :, cols] = acc_now[h, :, cols] * fade + part[:depth]
                sum_now[h, :, cols] = sum_now[h, :, cols] * fade + part[depth : depth + 1]
                block_max = later

        @pl.when(valid[ids[index]] == 0)
        def _():
            probs[slot] = jnp.zeros(probs.shape[1:], jnp.bfloat16)

        levels[seen + index] = max_now[...]
        copy_out(index).start()
    if last:
        log_two = math.log2(math.e)
        levels[seen + count] = max_now[...] + jnp.log(sum_now[...]) * log_two
        for h in range(heads):
            rows = slice(h * depth, (h + 1) * depth)
            attended[rows, :] = (acc_now[h] / sum_now[h]).astype(jnp.bfloat16)
        step = heads * depth
        half = projected.shape[0] // (2 * step)
        for place in range(2 * half):
            at = (place % 2) * half + place // 2
            part = mm(weight[:, at * step : (at + 1) * step], attended[...], TN)
            projected[place * step : (place + 1) * step, :] = part.astype(jnp.bfloat16)
    for index in range(max(0, count - 2), count):
        copy_out(index).wait()


def forward_call(ids, seen, valid, queries, pairs, state, weight, scale):
    count = len(ids)
    heads, tokens, depth = queries.shape
    f32, b16 = (jnp.float32, jnp.bfloat16)
    last = weight is not None
    row = jax.ShapeDtypeStruct((heads, 1, tokens), f32)
    outs = [pltpu.HBM((heads, tokens, tokens), b16)] * count
    levels_kind = pltpu.HBM if last else jax.ShapeDtypeStruct
    outs += [levels_kind((seen + count + last, heads, 1, tokens), f32), row, row]
    outs += [jax.ShapeDtypeStruct((heads, depth, tokens), f32)]
    operands = [valid, queries, *pairs] + (list(state) if seen else [])
    if last:
        operands += [weight]
        outs += [jax.ShapeDtypeStruct((heads * depth, tokens), b16)]
        outs += [pltpu.HBM((weight.shape[1], tokens), b16)]
    results = pl.pallas_call(
        functools.partial(forward_kernel, ids, seen, last, scale),
        out_shape=outs,
        in_specs=[SMEM] + [VMEM] * (len(operands) - 1),
        out_specs=[HBM] * count + [VMEM] * (len(outs) - count),
        scratch_shapes=[
            pltpu.VMEM((tokens, FORWARD_CHUNK), f32),
            pltpu.VMEM((tokens, FORWARD_CHUNK), f32),
            pltpu.VMEM((2, heads, tokens, tokens), b16),
            pltpu.SemaphoreType.DMA((2,)),
        ],
        compiler_params=pltpu.CompilerParams(vmem_limit_bytes=FORWARD_LIMIT),
        cost_estimate=FORWARD_COST,
        name="forward" + str(count),
    )(*operands)
    return (results[:count], results[count : count + 4], results[count + 4 :])


def middle_kernel(half, weight, gathered, attended, grads, terms):
    share = gathered.shape[0] // (2 * half)
    each = share // terms.shape[1]
    total = jnp.zeros(grads.shape, jnp.float32)
    for z in range(half):
        for x in range(2):
            block = gathered[(z * 2 + x) * share : (z * 2 + x + 1) * share, :]
            at = x * half + z
            total = total + mm(weight[:, at * share : (at + 1) * share], block)
            term = mm(block, attended[...], NT).astype(jnp.bfloat16)
            for e in range(each):
                terms[at * each + e] = term[e * terms.shape[1] : (e + 1) * terms.shape[1], :]
    grads[...] = total.astype(jnp.bfloat16)


def middle_call(half, shares, weight, gathered, attended):
    b16 = jnp.bfloat16
    rows, columns = weight.shape
    return pl.pallas_call(
        functools.partial(middle_kernel, half),
        out_shape=[
            jax.ShapeDtypeStruct(attended.shape, b16),
            pltpu.HBM((shares, columns // shares, rows), b16),
        ],
        in_specs=[VMEM] * 3,
        out_specs=[VMEM] * 2,
        compiler_params=pltpu.CompilerParams(vmem_limit_bytes=FORWARD_LIMIT),
        cost_estimate=BACKWARD_COST,
        name="middle",
    )(weight, pltpu.with_memory_space_constraint(gathered, pltpu.HBM), attended)


def backward_kernel(outputs, order, adds, extras, first, last, factor, *refs):
    ids = [i for group in outputs for i in group]
    count = len(ids)
    queries, grads, attended, levels = refs[:4]
    rest = refs[4:]
    pairs, prob_in, rest = (rest[:count], rest[count : 2 * count], rest[2 * count :])
    if not first:
        query_in, rest = (rest[0], rest[1:])
    added, rest = (rest[:extras], rest[extras:])
    outs, rest = (rest[: len(outputs)], rest[len(outputs) :])
    part_out = []
    for out, group in zip(outs, outputs):
        part_out += [out] if len(group) == 1 else [out.at[place] for place in range(len(group))]
    query_out, acc, grads_0, grads_1, probs, sems = rest
    score_grads = (grads_0, grads_1)
    heads, tokens, depth = queries.shape

    def copy_in(index, h):
        return pltpu.make_async_copy(prob_in[index].at[h], probs.at[index, h], sems.at[index, h])

    for index in range(count):
        for h in range(heads):
            copy_in(index, h).start()
    if first:
        acc[...] = jnp.zeros(acc.shape, jnp.float32)
    else:
        acc[...] = query_in[...]
    chains = [
        (index, h, c)
        for index in range(count)
        for h in range(heads)
        for c in range(0, tokens, BACKWARD_CHUNK)
    ]
    loads = [(index, h) for index in range(count) for h in range(heads)]
    waits = {(0, 0): loads[:1], (0, 1): loads[1:4], (2, 0): loads[4:]}
    rows = [slice(h * depth, (h + 1) * depth) for h in range(heads)]
    dots = []
    for h in range(heads):
        product = grads[rows[h], :].astype(jnp.float32) * attended[rows[h], :].astype(jnp.float32)
        dots.append(jnp.sum(product, axis=0, keepdims=True))
    grad, dot, turned = ({}, {}, {})

    def prob_grad(index, h, c):
        if c == 0:
            keep = jnp.exp2(levels[order[ids[index]], h] - levels[levels.shape[0] - 1, h])
            grad[index, h] = (grads[rows[h], :].astype(jnp.float32) * keep).astype(jnp.bfloat16)
            dot[index, h] = dots[h] * keep
            turned[index, h] = pairs[index][0, h].T
        return mm(pairs[index][1, h], grad[index, h][:, c : c + BACKWARD_CHUNK])

    def finish(index, kind, h, value):
        for which, at in adds[index]:
            ref = added[which]
            extra = ref[kind, h] if at is None else ref[at, kind, h]
            value = value + extra.astype(jnp.float32)
        part_out[index][kind, h] = value.astype(part_out[index].dtype)

    now = prob_grad(*chains[0])
    for place, (index, h, c) in enumerate(chains):
        cols = slice(c, c + BACKWARD_CHUNK)
        if place + 1 < len(chains):
            later = prob_grad(*chains[place + 1])
        if c == 0:
            for load in waits.get((index, h), ()):
                copy_in(*load).wait()
            finish(index, 1, h, mm(probs[index, h], grad[index, h], NT))
        weights = probs[index, h, :, cols].astype(jnp.float32)
        ds = (weights * (now - dot[index, h][:, cols])).astype(jnp.bfloat16)
        held = score_grads[(index * heads + h) % len(score_grads)]
        held[:, cols] = ds
        acc[h, :, cols] += mm(turned[index, h], ds)
        if c + BACKWARD_CHUNK == tokens:
            finish(index, 0, h, mm(held[...], queries[h]) * factor)
        now = later
    if last:
        for h in range(heads):
            query_out[h] = acc[h].T * factor
    else:
        query_out[...] = acc[...]


def backward_call(outputs, order, queries, grads, attended, levels, slabs, probs, query, added, last, factor):
    ids = [i for group in outputs for i in group]
    count = len(ids)
    heads, tokens, depth = queries.shape
    f32, b16 = (jnp.float32, jnp.bfloat16)
    first = query is None
    outs = []
    for group in outputs:
        several = () if len(group) == 1 else (len(group),)
        kind = jax.ShapeDtypeStruct if last else pltpu.HBM
        outs.append(kind(several + (2, heads, tokens, depth), f32 if last else b16))
    query_shape = (heads, tokens, depth) if last else (heads, depth, tokens)
    outs += [pltpu.HBM(query_shape, f32)]

    def in_hbm(value):
        return pltpu.with_memory_space_constraint(value, pltpu.HBM)

    operands = [queries, grads, attended, in_hbm(levels)]
    operands += [in_hbm(slabs[i]) if i == 0 else slabs[i] for i in ids]
    specs = [VMEM] * len(operands) + [HBM] * count
    operands += [in_hbm(probs[i]) for i in ids]
    operands += [] if first else [in_hbm(query)]
    arrays = []
    adds = []
    for terms in added:
        for term, _ in terms:
            if not any(term is array for array in arrays):
                arrays.append(term)
        which = [next(k for k, array in enumerate(arrays) if term is array) for term, _ in terms]
        adds.append(tuple((k, at) for k, (_, at) in zip(which, terms)))
    operands += arrays
    results = pl.pallas_call(
        functools.partial(backward_kernel, outputs, order, tuple(adds), len(arrays), first, last, factor),
        out_shape=outs,
        in_specs=specs + [VMEM] * (len(operands) - len(specs)),
        out_specs=[VMEM] * len(outs),
        scratch_shapes=[
            pltpu.VMEM((heads, depth, tokens), f32),
            pltpu.VMEM((tokens, tokens), b16),
            pltpu.VMEM((tokens, tokens), b16),
            pltpu.VMEM((count, heads, tokens, tokens), b16),
            pltpu.SemaphoreType.DMA((count, heads)),
        ],
        compiler_params=pltpu.CompilerParams(vmem_limit_bytes=BACKWARD_LIMIT),
        cost_estimate=BACKWARD_COST,
        name="backward" + str(count),
    )(*operands)
    return results


def sum_kernel(*refs):
    terms, outs = (refs[:-2], refs[-2:])
    for kind, out in enumerate(outs):
        whole = terms[0][kind]
        for term in terms[1:]:
            whole = whole + term[kind].astype(jnp.float32)
        out[...] = whole


def sum_call(*terms):
    shape = jax.ShapeDtypeStruct(terms[0].shape[1:], jnp.float32)
    return pl.pallas_call(
        sum_kernel,
        out_shape=[shape, shape],
        in_specs=[VMEM] * len(terms),
        out_specs=[VMEM, VMEM],
        compiler_params=pltpu.CompilerParams(vmem_limit_bytes=FORWARD_LIMIT),
        cost_estimate=BACKWARD_COST,
        name="sums",
    )(*terms)


def shards(query_rows, key_rows, value_rows, out_weight, out_grad):
    heads, _, _, tokens, depth = query_rows.shape
    factor = 1.0 / math.sqrt(depth)
    scale = factor * math.log2(math.e)
    times, rows = (lax.axis_size("tm"), lax.axis_size("height"))
    both = ("tm", "height")

    def grid(pairs):
        return [(a * rows + b, a2 * rows + b2) for (a, b), (a2, b2) in pairs]

    every = [(a, b) for a in range(times) for b in range(rows)]
    crossing = [a for a in range(times) if 0 <= (a - 1 if a % 2 == 0 else a + 1) < times]

    def across(a):
        return a - 1 if a % 2 == 0 else a + 1

    up = grid([((a, b), (a, b + 1)) for a, b in every if b + 1 < rows])
    down = grid([((a, b), (a, b - 1)) for a, b in every if b >= 1])
    partner = grid([((a, b), (a ^ 1, b)) for a, b in every])
    cross = grid([((a, b), (across(a), b)) for a, b in every if a in crossing])
    cross_up = grid([((a, b), (a, b + 1)) for a, b in every if a in crossing and b + 1 < rows])
    cross_down = grid([((a, b), (a, b - 1)) for a, b in every if a in crossing and b >= 1])

    def send(value, route):
        return lax.ppermute(value, both, route)

    time, row = (lax.axis_index("tm"), lax.axis_index("height"))
    other = jnp.where(time % 2 == 0, time - 1, time + 1)
    crossed = (other >= 0) & (other < times)
    above, below = (row > 0, row < rows - 1)
    yes = row >= 0
    valid = jnp.stack(
        [yes, above, below, yes, above, below, crossed, crossed & above, crossed & below]
    ).astype(jnp.int32)

    queries = query_rows[:, 0, 0]
    own = jnp.stack((key_rows[:, 0, 0], value_rows[:, 0, 0]))
    out_share = out_grad.shape[0]
    grad_flat = out_grad.reshape(out_share, tokens)
    half = lax.axis_size("head") // 2
    side = lax.axis_index("head") // half
    rings = [list(range(half)), list(range(half, 2 * half))]
    swap = [(i, (i + half) % (2 * half)) for i in range(2 * half)]
    swapped = lax.ppermute(grad_flat, "head", swap)
    blocks = jnp.where(
        side == 0, jnp.stack([grad_flat, swapped]), jnp.stack([swapped, grad_flat])
    ).reshape(2 * out_share, tokens)
    grad_all = lax.all_gather(blocks, "head", axis_index_groups=rings, axis=0, tiled=True)

    slabs, probs = ([None] * 9, [None] * 9)
    groups = ((0, 3), (1, 2, 6), (4, 5, 7, 8))
    order = {i: place for place, i in enumerate([i for ids in groups for i in ids])}

    def forward(ids, state):
        weight = out_weight if ids is groups[-1] else None
        got, state, extra = forward_call(
            ids, order[ids[0]], valid, queries, [slabs[i] for i in ids], state, weight, scale
        )
        for place, i in enumerate(ids):
            probs[i] = got[place]
        return (state, extra)

    slabs[0] = own
    slabs[6] = send(own, cross)
    slabs[1] = send(own, up)
    slabs[2] = send(own, down)
    slabs[3] = send(own, partner)
    state, _ = forward(groups[0], None)
    slabs[6], *state = lax.optimization_barrier((slabs[6], *state))

    slabs[7] = send(slabs[6], cross_up)
    slabs[8] = send(slabs[6], cross_down)
    slabs[4] = send(slabs[1], partner)
    slabs[5] = send(slabs[2], partner)
    state, _ = forward(groups[1], state)
    state, extra = forward(groups[2], state)
    attended, projected = extra
    levels = state[0]
    projected = lax.psum_scatter(
        projected, "head", scatter_dimension=0, axis_index_groups=rings, tiled=True
    )
    kept = lax.dynamic_slice_in_dim(projected, side * out_share, out_share, 0)
    given = lax.dynamic_slice_in_dim(projected, (1 - side) * out_share, out_share, 0)
    got = lax.ppermute(given, "head", swap)
    projected = (kept.astype(jnp.float32) + got.astype(jnp.float32)).astype(jnp.bfloat16)
    projected = projected.reshape(out_share, 1, 1, tokens)
    grads, weight_part = middle_call(half, times * rows, out_weight, grad_all, attended)
    weight_terms = lax.all_to_all(weight_part, both, 0, 0)

    def backward(outputs, query, added, last=False):
        return backward_call(
            outputs, order, queries, grads, attended, levels, slabs, probs, query, added, last, factor
        )

    part_7, part_8, part_near, part_3, query = backward(((7,), (8,), (4, 5), (3,)), None, [()] * 5)
    weight_terms, part_7, part_8, part_near, part_3 = lax.optimization_barrier(
        (weight_terms, part_7, part_8, part_near, part_3)
    )
    weight_grad = jnp.sum(weight_terms.astype(jnp.float32), axis=0).T
    back_up = send(part_7, cross_down)
    back_down = send(part_8, cross_up)
    near = send(part_near, partner)
    near_own = send(part_3, partner)
    part_6, part_1, part_2, query = backward(
        ((6,), (1,), (2,)), query, [((back_up, None), (back_down, None)), ((near, 0),), ((near, 1),)]
    )
    far = send(part_6, cross)
    to_up = send(part_1, down)
    to_down = send(part_2, up)
    part_0, query_grad = backward(((0,),), query, [((near_own, None),)], True)
    projected, weight_grad, part_0 = lax.optimization_barrier((projected, weight_grad, part_0))
    owned = sum_call(part_0, far, to_up, to_down)
    grad_shape = (heads, 1, 1, tokens, depth)
    return (
        projected,
        query_grad.reshape(grad_shape),
        owned[0].reshape(grad_shape),
        owned[1].reshape(grad_shape),
        weight_grad,
    )


def solution(mesh):
    rows = P("head", "tm", "height", None, None)
    columns = P("head", "tm", "height", None)
    return jax.shard_map(
        shards,
        mesh=mesh,
        in_specs=(rows, rows, rows, P("head", None), columns),
        out_specs=(columns, rows, rows, rows, P("head", ("tm", "height"))),
        check_vma=False,
    )
```

```python
import functools
import math

import jax
import jax.numpy as jnp
from jax import lax
from jax.experimental import pallas as pl
from jax.experimental.pallas import tpu as pltpu
from jax.sharding import PartitionSpec as P

FORWARD_CHUNK = 256
BACKWARD_CHUNK = 256
VMEM = pl.BlockSpec(memory_space=pltpu.VMEM)
HBM = pl.BlockSpec(memory_space=pltpu.HBM)
SMEM = pl.BlockSpec(memory_space=pltpu.SMEM)
FORWARD_COST = pl.CostEstimate(flops=30 * 10**9, bytes_accessed=1000, transcendentals=0)
BACKWARD_COST = pl.CostEstimate(flops=1000000, bytes_accessed=1000, transcendentals=0)
LOWEST = -1e30
NT = (((1,), (1,)), ((), ()))
NN = (((1,), (0,)), ((), ()))
TN = (((0,), (0,)), ((), ()))
FORWARD_LIMIT = 24 * 1024 * 1024
BACKWARD_LIMIT = 34 * 1024 * 1024


def mm(a, b, dims=NN):
    return lax.dot_general(a, b, dims, preferred_element_type=jnp.float32)


def forward_kernel(ids, seen, last, scale, *refs):
    count = len(ids)
    valid, queries = refs[:2]
    pairs = refs[2 : 2 + count]
    rest = refs[2 + count :]
    if seen:
        levels_in, max_in, sum_in, acc_in = rest[:4]
        rest = rest[4:]
    if last:
        weight, rest = (rest[0], rest[1:])
    prob_out = rest[:count]
    levels, max_now, sum_now, acc_now = rest[count : count + 4]
    rest = rest[count + 4 :]
    if last:
        attended, projected, rest = (rest[0], rest[1], rest[2:])
    scores, probs, sems = (rest[:2], rest[2], rest[3])
    heads, tokens, depth = queries.shape
    if seen:
        levels[:seen] = levels_in[...]
        max_now[...] = max_in[...]
        sum_now[...] = sum_in[...]
        acc_now[...] = acc_in[...]
    else:
        max_now[...] = jnp.full(max_now.shape, LOWEST, jnp.float32)
        sum_now[...] = jnp.zeros(sum_now.shape, jnp.float32)
        acc_now[...] = jnp.zeros(acc_now.shape, jnp.float32)
    chains = [(h, c) for h in range(heads) for c in range(0, tokens, FORWARD_CHUNK)]

    def copy_out(index):
        return pltpu.make_async_copy(probs.at[index % 2], prob_out[index], sems.at[index % 2])

    for index in range(count):
        slot = index % 2
        if index >= 2:
            copy_out(index - 2).wait()

        @pl.when(valid[ids[index]] > 0)
        def _():
            pair = pairs[index]
            ones = jnp.ones((16, tokens), jnp.bfloat16)
            values = [jnp.concatenate([pair[1, h].T, ones], axis=0) for h in range(heads)]

            def score(place):
                h, c = chains[place]
                s = mm(pair[0, h], queries[h, c : c + FORWARD_CHUNK, :], NT)
                scores[place % 2][...] = s
                return jnp.max(s, axis=0, keepdims=True) * scale

            block_max = score(0)
            for place, (h, c) in enumerate(chains):
                cols = slice(c, c + FORWARD_CHUNK)
                if place + 1 < len(chains):
                    later = score(place + 1)
                before = max_now[h, :, cols]
                now = jnp.maximum(before, block_max)
                p = jnp.exp2(scores[place % 2][...] * scale - now).astype(jnp.bfloat16)
                probs[slot, h, :, cols] = p
                part = mm(values[h], p)
                fade = jnp.exp2(before - now)
                max_now[h, :, cols] = now
                acc_now[h, :, cols] = acc_now[h, :, cols] * fade + part[:depth]
                sum_now[h, :, cols] = sum_now[h, :, cols] * fade + part[depth : depth + 1]
                block_max = later

        @pl.when(valid[ids[index]] == 0)
        def _():
            probs[slot] = jnp.zeros(probs.shape[1:], jnp.bfloat16)

        levels[seen + index] = max_now[...]
        copy_out(index).start()
    if last:
        log_two = math.log2(math.e)
        levels[seen + count] = max_now[...] + jnp.log(sum_now[...]) * log_two
        for h in range(heads):
            rows = slice(h * depth, (h + 1) * depth)
            attended[rows, :] = (acc_now[h] / sum_now[h]).astype(jnp.bfloat16)
        step = heads * depth
        half = projected.shape[0] // (2 * step)
        for place in range(2 * half):
            at = (place % 2) * half + place // 2
            part = mm(weight[:, at * step : (at + 1) * step], attended[...], TN)
            projected[place * step : (place + 1) * step, :] = part.astype(jnp.bfloat16)
    for index in range(max(0, count - 2), count):
        copy_out(index).wait()


def forward_call(ids, seen, valid, queries, pairs, state, weight, scale):
    count = len(ids)
    heads, tokens, depth = queries.shape
    f32, b16 = (jnp.float32, jnp.bfloat16)
    last = weight is not None
    row = jax.ShapeDtypeStruct((heads, 1, tokens), f32)
    outs = [pltpu.HBM((heads, tokens, tokens), b16)] * count
    levels_kind = pltpu.HBM if last else jax.ShapeDtypeStruct
    outs += [levels_kind((seen + count + last, heads, 1, tokens), f32), row, row]
    outs += [jax.ShapeDtypeStruct((heads, depth, tokens), f32)]
    operands = [valid, queries, *pairs] + (list(state) if seen else [])
    if last:
        operands += [weight]
        outs += [jax.ShapeDtypeStruct((heads * depth, tokens), b16)]
        outs += [pltpu.HBM((weight.shape[1], tokens), b16)]
    results = pl.pallas_call(
        functools.partial(forward_kernel, ids, seen, last, scale),
        out_shape=outs,
        in_specs=[SMEM] + [VMEM] * (len(operands) - 1),
        out_specs=[HBM] * count + [VMEM] * (len(outs) - count),
        scratch_shapes=[
            pltpu.VMEM((tokens, FORWARD_CHUNK), f32),
            pltpu.VMEM((tokens, FORWARD_CHUNK), f32),
            pltpu.VMEM((2, heads, tokens, tokens), b16),
            pltpu.SemaphoreType.DMA((2,)),
        ],
        compiler_params=pltpu.CompilerParams(vmem_limit_bytes=FORWARD_LIMIT),
        cost_estimate=FORWARD_COST,
        name="forward" + str(count),
    )(*operands)
    return (results[:count], results[count : count + 4], results[count + 4 :])


def middle_kernel(half, weight, gathered, attended, grads, terms):
    share = gathered.shape[0] // (2 * half)
    each = share // terms.shape[1]
    total = jnp.zeros(grads.shape, jnp.float32)
    for z in range(half):
        for x in range(2):
            block = gathered[(z * 2 + x) * share : (z * 2 + x + 1) * share, :]
            at = x * half + z
            total = total + mm(weight[:, at * share : (at + 1) * share], block)
            term = mm(block, attended[...], NT).astype(jnp.bfloat16)
            for e in range(each):
                terms[at * each + e] = term[e * terms.shape[1] : (e + 1) * terms.shape[1], :]
    grads[...] = total.astype(jnp.bfloat16)


def middle_call(half, shares, weight, gathered, attended):
    b16 = jnp.bfloat16
    rows, columns = weight.shape
    return pl.pallas_call(
        functools.partial(middle_kernel, half),
        out_shape=[
            jax.ShapeDtypeStruct(attended.shape, b16),
            pltpu.HBM((shares, columns // shares, rows), b16),
        ],
        in_specs=[VMEM] * 3,
        out_specs=[VMEM] * 2,
        compiler_params=pltpu.CompilerParams(vmem_limit_bytes=FORWARD_LIMIT),
        cost_estimate=BACKWARD_COST,
        name="middle",
    )(weight, pltpu.with_memory_space_constraint(gathered, pltpu.HBM), attended)


def backward_kernel(outputs, order, adds, extras, first, last, factor, *refs):
    ids = [i for group in outputs for i in group]
    count = len(ids)
    queries, grads, attended, levels = refs[:4]
    rest = refs[4:]
    pairs, prob_in, rest = (rest[:count], rest[count : 2 * count], rest[2 * count :])
    if not first:
        query_in, rest = (rest[0], rest[1:])
    added, rest = (rest[:extras], rest[extras:])
    outs, rest = (rest[: len(outputs)], rest[len(outputs) :])
    part_out = []
    for out, group in zip(outs, outputs):
        part_out += [out] if len(group) == 1 else [out.at[place] for place in range(len(group))]
    query_out, acc, grads_0, grads_1, probs, sems = rest
    score_grads = (grads_0, grads_1)
    heads, tokens, depth = queries.shape

    def copy_in(index, h):
        return pltpu.make_async_copy(prob_in[index].at[h], probs.at[index, h], sems.at[index, h])

    for index in range(count):
        for h in range(heads):
            copy_in(index, h).start()
    if first:
        acc[...] = jnp.zeros(acc.shape, jnp.float32)
    else:
        acc[...] = query_in[...]
    chains = [
        (index, h, c)
        for index in range(count)
        for h in range(heads)
        for c in range(0, tokens, BACKWARD_CHUNK)
    ]
    loads = [(index, h) for index in range(count) for h in range(heads)]
    waits = {(0, 0): loads[:1], (0, 1): loads[1:4], (2, 0): loads[4:]}
    rows = [slice(h * depth, (h + 1) * depth) for h in range(heads)]
    dots = []
    for h in range(heads):
        product = grads[rows[h], :].astype(jnp.float32) * attended[rows[h], :].astype(jnp.float32)
        dots.append(jnp.sum(product, axis=0, keepdims=True))
    grad, dot, turned = ({}, {}, {})

    def prob_grad(index, h, c):
        if c == 0:
            keep = jnp.exp2(levels[order[ids[index]], h] - levels[levels.shape[0] - 1, h])
            grad[index, h] = (grads[rows[h], :].astype(jnp.float32) * keep).astype(jnp.bfloat16)
            dot[index, h] = dots[h] * keep
            turned[index, h] = pairs[index][0, h].T
        return mm(pairs[index][1, h], grad[index, h][:, c : c + BACKWARD_CHUNK])

    def finish(index, kind, h, value):
        for which, at in adds[index]:
            ref = added[which]
            extra = ref[kind, h] if at is None else ref[at, kind, h]
            value = value + extra.astype(jnp.float32)
        part_out[index][kind, h] = value.astype(part_out[index].dtype)

    now = prob_grad(*chains[0])
    for place, (index, h, c) in enumerate(chains):
        cols = slice(c, c + BACKWARD_CHUNK)
        if place + 1 < len(chains):
            later = prob_grad(*chains[place + 1])
        if c == 0:
            for load in waits.get((index, h), ()):
                copy_in(*load).wait()
            finish(index, 1, h, mm(probs[index, h], grad[index, h], NT))
        weights = probs[index, h, :, cols].astype(jnp.float32)
        ds = (weights * (now - dot[index, h][:, cols])).astype(jnp.bfloat16)
        held = score_grads[(index * heads + h) % len(score_grads)]
        held[:, cols] = ds
        acc[h, :, cols] += mm(turned[index, h], ds)
        if c + BACKWARD_CHUNK == tokens:
            finish(index, 0, h, mm(held[...], queries[h]) * factor)
        now = later
    if last:
        for h in range(heads):
            query_out[h] = acc[h].T * factor
    else:
        query_out[...] = acc[...]


def backward_call(outputs, order, queries, grads, attended, levels, slabs, probs, query, added, last, factor):
    ids = [i for group in outputs for i in group]
    count = len(ids)
    heads, tokens, depth = queries.shape
    f32, b16 = (jnp.float32, jnp.bfloat16)
    first = query is None
    outs = []
    for group in outputs:
        several = () if len(group) == 1 else (len(group),)
        kind = jax.ShapeDtypeStruct if last else pltpu.HBM
        outs.append(kind(several + (2, heads, tokens, depth), f32 if last else b16))
    query_shape = (heads, tokens, depth) if last else (heads, depth, tokens)
    outs += [pltpu.HBM(query_shape, f32)]

    def in_hbm(value):
        return pltpu.with_memory_space_constraint(value, pltpu.HBM)

    operands = [queries, grads, attended, in_hbm(levels)]
    operands += [slabs[i] if i in (1, 2, 6) else in_hbm(slabs[i]) for i in ids]
    specs = [VMEM] * len(operands) + [HBM] * count
    operands += [in_hbm(probs[i]) for i in ids]
    operands += [] if first else [in_hbm(query)]
    arrays = []
    adds = []
    for terms in added:
        for term, _ in terms:
            if not any(term is array for array in arrays):
                arrays.append(term)
        which = [next(k for k, array in enumerate(arrays) if term is array) for term, _ in terms]
        adds.append(tuple((k, at) for k, (_, at) in zip(which, terms)))
    operands += arrays
    results = pl.pallas_call(
        functools.partial(backward_kernel, outputs, order, tuple(adds), len(arrays), first, last, factor),
        out_shape=outs,
        in_specs=specs + [VMEM] * (len(operands) - len(specs)),
        out_specs=[VMEM] * len(outs),
        scratch_shapes=[
            pltpu.VMEM((heads, depth, tokens), f32),
            pltpu.VMEM((tokens, tokens), b16),
            pltpu.VMEM((tokens, tokens), b16),
            pltpu.VMEM((count, heads, tokens, tokens), b16),
            pltpu.SemaphoreType.DMA((count, heads)),
        ],
        compiler_params=pltpu.CompilerParams(vmem_limit_bytes=BACKWARD_LIMIT),
        cost_estimate=BACKWARD_COST,
        name="backward" + str(count),
    )(*operands)
    return results


def sum_kernel(*refs):
    terms, outs = (refs[:-2], refs[-2:])
    for kind, out in enumerate(outs):
        whole = terms[0][kind]
        for term in terms[1:]:
            whole = whole + term[kind].astype(jnp.float32)
        out[...] = whole


def sum_call(*terms):
    shape = jax.ShapeDtypeStruct(terms[0].shape[1:], jnp.float32)
    return pl.pallas_call(
        sum_kernel,
        out_shape=[shape, shape],
        in_specs=[VMEM] * len(terms),
        out_specs=[VMEM, VMEM],
        compiler_params=pltpu.CompilerParams(vmem_limit_bytes=FORWARD_LIMIT),
        cost_estimate=BACKWARD_COST,
        name="sums",
    )(*terms)


def shards(query_rows, key_rows, value_rows, out_weight, out_grad):
    heads, _, _, tokens, depth = query_rows.shape
    factor = 1.0 / math.sqrt(depth)
    scale = factor * math.log2(math.e)
    times, rows = (lax.axis_size("tm"), lax.axis_size("height"))
    both = ("tm", "height")

    def grid(pairs):
        return [(a * rows + b, a2 * rows + b2) for (a, b), (a2, b2) in pairs]

    every = [(a, b) for a in range(times) for b in range(rows)]
    crossing = [a for a in range(times) if 0 <= (a - 1 if a % 2 == 0 else a + 1) < times]

    def across(a):
        return a - 1 if a % 2 == 0 else a + 1

    up = grid([((a, b), (a, b + 1)) for a, b in every if b + 1 < rows])
    down = grid([((a, b), (a, b - 1)) for a, b in every if b >= 1])
    partner = grid([((a, b), (a ^ 1, b)) for a, b in every])
    cross = grid([((a, b), (across(a), b)) for a, b in every if a in crossing])
    cross_up = grid([((a, b), (a, b + 1)) for a, b in every if a in crossing and b + 1 < rows])
    cross_down = grid([((a, b), (a, b - 1)) for a, b in every if a in crossing and b >= 1])

    def send(value, route):
        return lax.ppermute(value, both, route)

    time, row = (lax.axis_index("tm"), lax.axis_index("height"))
    other = jnp.where(time % 2 == 0, time - 1, time + 1)
    crossed = (other >= 0) & (other < times)
    above, below = (row > 0, row < rows - 1)
    yes = row >= 0
    valid = jnp.stack(
        [yes, above, below, yes, above, below, crossed, crossed & above, crossed & below]
    ).astype(jnp.int32)

    queries = query_rows[:, 0, 0]
    own = jnp.stack((key_rows[:, 0, 0], value_rows[:, 0, 0]))
    out_share = out_grad.shape[0]
    grad_flat = out_grad.reshape(out_share, tokens)
    half = lax.axis_size("head") // 2
    side = lax.axis_index("head") // half
    rings = [list(range(half)), list(range(half, 2 * half))]
    swap = [(i, (i + half) % (2 * half)) for i in range(2 * half)]
    swapped = lax.ppermute(grad_flat, "head", swap)
    blocks = jnp.where(
        side == 0, jnp.stack([grad_flat, swapped]), jnp.stack([swapped, grad_flat])
    ).reshape(2 * out_share, tokens)
    grad_all = lax.all_gather(blocks, "head", axis_index_groups=rings, axis=0, tiled=True)

    slabs, probs = ([None] * 9, [None] * 9)
    groups = ((0, 3), (1, 2, 6), (4, 5, 7, 8))
    order = {i: place for place, i in enumerate([i for ids in groups for i in ids])}

    def forward(ids, state):
        weight = out_weight if ids is groups[-1] else None
        got, state, extra = forward_call(
            ids, order[ids[0]], valid, queries, [slabs[i] for i in ids], state, weight, scale
        )
        for place, i in enumerate(ids):
            probs[i] = got[place]
        return (state, extra)

    slabs[0] = own
    slabs[6] = send(own, cross)
    slabs[1] = send(own, up)
    slabs[2] = send(own, down)
    slabs[3] = send(own, partner)
    state, _ = forward(groups[0], None)
    slabs[6], *state = lax.optimization_barrier((slabs[6], *state))

    slabs[7] = send(slabs[6], cross_up)
    slabs[8] = send(slabs[6], cross_down)
    slabs[4] = send(slabs[1], partner)
    slabs[5] = send(slabs[2], partner)
    state, _ = forward(groups[1], state)
    state, extra = forward(groups[2], state)
    attended, projected = extra
    levels = state[0]
    projected = lax.psum_scatter(
        projected, "head", scatter_dimension=0, axis_index_groups=rings, tiled=True
    )
    kept = lax.dynamic_slice_in_dim(projected, side * out_share, out_share, 0)
    given = lax.dynamic_slice_in_dim(projected, (1 - side) * out_share, out_share, 0)
    grads, weight_part = middle_call(half, times * rows, out_weight, grad_all, attended)
    weight_terms = lax.all_to_all(weight_part, both, 0, 0)

    def backward(outputs, query, added, last=False):
        return backward_call(
            outputs, order, queries, grads, attended, levels, slabs, probs, query, added, last, factor
        )

    part_7, part_8, query = backward(((7,), (8,)), None, [(), ()])
    back_up = send(part_7, cross_down)
    back_down = send(part_8, cross_up)
    part_near, part_3, query = backward(((4, 5), (3,)), query, [(), (), ()])
    weight_terms, back_up, back_down, part_near, part_3, query = lax.optimization_barrier(
        (weight_terms, back_up, back_down, part_near, part_3, query)
    )
    near = send(part_near, partner)
    near_own = send(part_3, partner)
    weight_grad = jnp.sum(weight_terms.astype(jnp.float32), axis=0).T
    kept, given, weight_grad, query = lax.optimization_barrier((kept, given, weight_grad, query))
    got = lax.ppermute(given, "head", swap)
    projected = (kept.astype(jnp.float32) + got.astype(jnp.float32)).astype(jnp.bfloat16)
    projected = projected.reshape(out_share, 1, 1, tokens)
    part_6, part_1, part_2, query = backward(
        ((6,), (1,), (2,)), query, [((back_up, None), (back_down, None)), ((near, 0),), ((near, 1),)]
    )
    far = send(part_6, cross)
    to_up = send(part_1, down)
    to_down = send(part_2, up)
    part_0, query_grad = backward(((0,),), query, [((near_own, None),)], True)
    projected, part_0 = lax.optimization_barrier((projected, part_0))
    owned = sum_call(part_0, far, to_up, to_down)
    grad_shape = (heads, 1, 1, tokens, depth)
    return (
        projected,
        query_grad.reshape(grad_shape),
        owned[0].reshape(grad_shape),
        owned[1].reshape(grad_shape),
        weight_grad,
    )


def solution(mesh):
    rows = P("head", "tm", "height", None, None)
    columns = P("head", "tm", "height", None)
    return jax.shard_map(
        shards,
        mesh=mesh,
        in_specs=(rows, rows, rows, P("head", None), columns),
        out_specs=(columns, rows, rows, rows, P("head", ("tm", "height"))),
        check_vma=False,
    )
```

```python
import functools
import math

import jax
import jax.numpy as jnp
from jax import lax
from jax.experimental import pallas as pl
from jax.experimental.pallas import tpu as pltpu
from jax.sharding import PartitionSpec as P

FORWARD_CHUNK = 256
BACKWARD_CHUNK = 256
VMEM = pl.BlockSpec(memory_space=pltpu.VMEM)
HBM = pl.BlockSpec(memory_space=pltpu.HBM)
SMEM = pl.BlockSpec(memory_space=pltpu.SMEM)
FORWARD_COST = pl.CostEstimate(flops=30 * 10**9, bytes_accessed=1000, transcendentals=0)
BACKWARD_COST = pl.CostEstimate(flops=1000000, bytes_accessed=1000, transcendentals=0)
LOWEST = -1e30
SIDE = 9
NT = (((1,), (1,)), ((), ()))
NN = (((1,), (0,)), ((), ()))
TN = (((0,), (0,)), ((), ()))
FORWARD_LIMIT = 24 * 1024 * 1024
BACKWARD_LIMIT = 34 * 1024 * 1024


def mm(a, b, dims=NN):
    return lax.dot_general(a, b, dims, preferred_element_type=jnp.float32)


def forward_kernel(ids, seen, last, scale, *refs):
    count = len(ids)
    valid, queries = refs[:2]
    pairs = refs[2 : 2 + count]
    rest = refs[2 + count :]
    if seen:
        levels_in, max_in, sum_in, acc_in = rest[:4]
        rest = rest[4:]
    if last:
        weight, rest = (rest[0], rest[1:])
    prob_out = rest[:count]
    levels, max_now, sum_now, acc_now = rest[count : count + 4]
    rest = rest[count + 4 :]
    if last:
        attended, projected, rest = (rest[0], rest[1], rest[2:])
    scores, probs, sems = (rest[:2], rest[2], rest[3])
    heads, tokens, depth = queries.shape
    if seen:
        levels[:seen] = levels_in[...]
        max_now[...] = max_in[...]
        sum_now[...] = sum_in[...]
        acc_now[...] = acc_in[...]
    else:
        max_now[...] = jnp.full(max_now.shape, LOWEST, jnp.float32)
        sum_now[...] = jnp.zeros(sum_now.shape, jnp.float32)
        acc_now[...] = jnp.zeros(acc_now.shape, jnp.float32)
    chains = [(h, c) for h in range(heads) for c in range(0, tokens, FORWARD_CHUNK)]

    def copy_out(index):
        return pltpu.make_async_copy(probs.at[index % 2], prob_out[index], sems.at[index % 2])

    for index in range(count):
        slot = index % 2
        if index >= 2:
            copy_out(index - 2).wait()

        @pl.when(valid[ids[index]] > 0)
        def _():
            pair = pairs[index]
            ones = jnp.ones((16, tokens), jnp.bfloat16)
            values = [jnp.concatenate([pair[1, h].T, ones], axis=0) for h in range(heads)]

            def score(place):
                h, c = chains[place]
                s = mm(pair[0, h], queries[h, c : c + FORWARD_CHUNK, :], NT)
                scores[place % 2][...] = s
                return jnp.max(s, axis=0, keepdims=True) * scale

            block_max = score(0)
            for place, (h, c) in enumerate(chains):
                cols = slice(c, c + FORWARD_CHUNK)
                if place + 1 < len(chains):
                    later = score(place + 1)
                before = max_now[h, :, cols]
                now = jnp.maximum(before, block_max)
                p = jnp.exp2(scores[place % 2][...] * scale - now).astype(jnp.bfloat16)
                probs[slot, h, :, cols] = p
                part = mm(values[h], p)
                fade = jnp.exp2(before - now)
                max_now[h, :, cols] = now
                acc_now[h, :, cols] = acc_now[h, :, cols] * fade + part[:depth]
                sum_now[h, :, cols] = sum_now[h, :, cols] * fade + part[depth : depth + 1]
                block_max = later

        @pl.when(valid[ids[index]] == 0)
        def _():
            probs[slot] = jnp.zeros(probs.shape[1:], jnp.bfloat16)

        levels[seen + index] = max_now[...]
        copy_out(index).start()
    if last:
        log_two = math.log2(math.e)
        levels[seen + count] = max_now[...] + jnp.log(sum_now[...]) * log_two
        for h in range(heads):
            rows = slice(h * depth, (h + 1) * depth)
            attended[rows, :] = (acc_now[h] / sum_now[h]).astype(jnp.bfloat16)
        step = heads * depth
        half = projected.shape[0] // (2 * step)
        for place in range(2 * half):
            x = valid[SIDE] if place % 2 == 0 else 1 - valid[SIDE]
            start = pl.multiple_of((x * half + place // 2) * step, step)
            part = mm(weight[:, pl.ds(start, step)], attended[...], TN)
            projected[place * step : (place + 1) * step, :] = part.astype(jnp.bfloat16)
    for index in range(max(0, count - 2), count):
        copy_out(index).wait()


def forward_call(ids, seen, valid, queries, pairs, state, weight, scale):
    count = len(ids)
    heads, tokens, depth = queries.shape
    f32, b16 = (jnp.float32, jnp.bfloat16)
    last = weight is not None
    row = jax.ShapeDtypeStruct((heads, 1, tokens), f32)
    outs = [pltpu.HBM((heads, tokens, tokens), b16)] * count
    levels_kind = pltpu.HBM if last else jax.ShapeDtypeStruct
    outs += [levels_kind((seen + count + last, heads, 1, tokens), f32), row, row]
    outs += [jax.ShapeDtypeStruct((heads, depth, tokens), f32)]
    operands = [valid, queries, *pairs] + (list(state) if seen else [])
    if last:
        operands += [weight]
        outs += [jax.ShapeDtypeStruct((heads * depth, tokens), b16)]
        outs += [pltpu.HBM((weight.shape[1], tokens), b16)]
    results = pl.pallas_call(
        functools.partial(forward_kernel, ids, seen, last, scale),
        out_shape=outs,
        in_specs=[SMEM] + [VMEM] * (len(operands) - 1),
        out_specs=[HBM] * count + [VMEM] * (len(outs) - count),
        scratch_shapes=[
            pltpu.VMEM((tokens, FORWARD_CHUNK), f32),
            pltpu.VMEM((tokens, FORWARD_CHUNK), f32),
            pltpu.VMEM((2, heads, tokens, tokens), b16),
            pltpu.SemaphoreType.DMA((2,)),
        ],
        compiler_params=pltpu.CompilerParams(vmem_limit_bytes=FORWARD_LIMIT),
        cost_estimate=FORWARD_COST,
        name="forward" + str(count),
    )(*operands)
    return (results[:count], results[count : count + 4], results[count + 4 :])


def middle_kernel(half, weight, gathered, attended, grads, terms):
    share = gathered.shape[0] // (2 * half)
    each = share // terms.shape[1]
    total = jnp.zeros(grads.shape, jnp.float32)
    for z in range(half):
        for x in range(2):
            block = gathered[(z * 2 + x) * share : (z * 2 + x + 1) * share, :]
            at = x * half + z
            total = total + mm(weight[:, at * share : (at + 1) * share], block)
            term = mm(block, attended[...], NT).astype(jnp.bfloat16)
            for e in range(each):
                terms[at * each + e] = term[e * terms.shape[1] : (e + 1) * terms.shape[1], :]
    grads[...] = total.astype(jnp.bfloat16)


def middle_call(half, shares, weight, gathered, attended):
    b16 = jnp.bfloat16
    rows, columns = weight.shape
    return pl.pallas_call(
        functools.partial(middle_kernel, half),
        out_shape=[
            jax.ShapeDtypeStruct(attended.shape, b16),
            pltpu.HBM((shares, columns // shares, rows), b16),
        ],
        in_specs=[VMEM] * 3,
        out_specs=[VMEM] * 2,
        compiler_params=pltpu.CompilerParams(vmem_limit_bytes=FORWARD_LIMIT),
        cost_estimate=BACKWARD_COST,
        name="middle",
    )(weight, pltpu.with_memory_space_constraint(gathered, pltpu.HBM), attended)


def backward_kernel(outputs, order, adds, extras, first, last, factor, *refs):
    ids = [i for group in outputs for i in group]
    count = len(ids)
    queries, grads, attended, levels = refs[:4]
    rest = refs[4:]
    pairs, prob_in, rest = (rest[:count], rest[count : 2 * count], rest[2 * count :])
    if not first:
        query_in, rest = (rest[0], rest[1:])
    added, rest = (rest[:extras], rest[extras:])
    outs, rest = (rest[: len(outputs)], rest[len(outputs) :])
    part_out = []
    for out, group in zip(outs, outputs):
        part_out += [out] if len(group) == 1 else [out.at[place] for place in range(len(group))]
    query_out, acc, grads_0, grads_1, probs, sems = rest
    score_grads = (grads_0, grads_1)
    heads, tokens, depth = queries.shape

    def copy_in(index, h):
        return pltpu.make_async_copy(prob_in[index].at[h], probs.at[index, h], sems.at[index, h])

    for index in range(count):
        for h in range(heads):
            copy_in(index, h).start()
    if first:
        acc[...] = jnp.zeros(acc.shape, jnp.float32)
    else:
        acc[...] = query_in[...]
    chains = [
        (index, h, c)
        for index in range(count)
        for h in range(heads)
        for c in range(0, tokens, BACKWARD_CHUNK)
    ]
    loads = [(index, h) for index in range(count) for h in range(heads)]
    waits = {(0, 0): loads[:1], (0, 1): loads[1:4], (2, 0): loads[4:]}
    rows = [slice(h * depth, (h + 1) * depth) for h in range(heads)]
    dots = []
    for h in range(heads):
        product = grads[rows[h], :].astype(jnp.float32) * attended[rows[h], :].astype(jnp.float32)
        dots.append(jnp.sum(product, axis=0, keepdims=True))
    grad, dot, turned = ({}, {}, {})

    def prob_grad(index, h, c):
        if c == 0:
            keep = jnp.exp2(levels[order[ids[index]], h] - levels[levels.shape[0] - 1, h])
            grad[index, h] = (grads[rows[h], :].astype(jnp.float32) * keep).astype(jnp.bfloat16)
            dot[index, h] = dots[h] * keep
            turned[index, h] = pairs[index][0, h].T
        return mm(pairs[index][1, h], grad[index, h][:, c : c + BACKWARD_CHUNK])

    def finish(index, kind, h, value):
        for which, at in adds[index]:
            ref = added[which]
            extra = ref[kind, h] if at is None else ref[at, kind, h]
            value = value + extra.astype(jnp.float32)
        part_out[index][kind, h] = value.astype(part_out[index].dtype)

    now = prob_grad(*chains[0])
    for place, (index, h, c) in enumerate(chains):
        cols = slice(c, c + BACKWARD_CHUNK)
        if place + 1 < len(chains):
            later = prob_grad(*chains[place + 1])
        if c == 0:
            for load in waits.get((index, h), ()):
                copy_in(*load).wait()
            finish(index, 1, h, mm(probs[index, h], grad[index, h], NT))
        weights = probs[index, h, :, cols].astype(jnp.float32)
        ds = (weights * (now - dot[index, h][:, cols])).astype(jnp.bfloat16)
        held = score_grads[(index * heads + h) % len(score_grads)]
        held[:, cols] = ds
        acc[h, :, cols] += mm(turned[index, h], ds)
        if c + BACKWARD_CHUNK == tokens:
            finish(index, 0, h, mm(held[...], queries[h]) * factor)
        now = later
    if last:
        for h in range(heads):
            query_out[h] = acc[h].T * factor
    else:
        query_out[...] = acc[...]


def backward_call(outputs, order, queries, grads, attended, levels, slabs, probs, query, added, last, factor):
    ids = [i for group in outputs for i in group]
    count = len(ids)
    heads, tokens, depth = queries.shape
    f32, b16 = (jnp.float32, jnp.bfloat16)
    first = query is None
    outs = []
    for group in outputs:
        several = () if len(group) == 1 else (len(group),)
        kind = jax.ShapeDtypeStruct if last else pltpu.HBM
        outs.append(kind(several + (2, heads, tokens, depth), f32 if last else b16))
    query_shape = (heads, tokens, depth) if last else (heads, depth, tokens)
    outs += [pltpu.HBM(query_shape, f32)]

    def in_hbm(value):
        return pltpu.with_memory_space_constraint(value, pltpu.HBM)

    operands = [queries, grads, attended, in_hbm(levels)]
    operands += [slabs[i] if i in (1, 2, 6) else in_hbm(slabs[i]) for i in ids]
    specs = [VMEM] * len(operands) + [HBM] * count
    operands += [in_hbm(probs[i]) for i in ids]
    operands += [] if first else [in_hbm(query)]
    arrays = []
    adds = []
    for terms in added:
        for term, _ in terms:
            if not any(term is array for array in arrays):
                arrays.append(term)
        which = [next(k for k, array in enumerate(arrays) if term is array) for term, _ in terms]
        adds.append(tuple((k, at) for k, (_, at) in zip(which, terms)))
    operands += [in_hbm(array) for array in arrays]
    results = pl.pallas_call(
        functools.partial(backward_kernel, outputs, order, tuple(adds), len(arrays), first, last, factor),
        out_shape=outs,
        in_specs=specs + [VMEM] * (len(operands) - len(specs)),
        out_specs=[VMEM] * len(outs),
        scratch_shapes=[
            pltpu.VMEM((heads, depth, tokens), f32),
            pltpu.VMEM((tokens, tokens), b16),
            pltpu.VMEM((tokens, tokens), b16),
            pltpu.VMEM((count, heads, tokens, tokens), b16),
            pltpu.SemaphoreType.DMA((count, heads)),
        ],
        compiler_params=pltpu.CompilerParams(vmem_limit_bytes=BACKWARD_LIMIT),
        cost_estimate=BACKWARD_COST,
        name="backward" + str(count),
    )(*operands)
    return results


def sum_kernel(*refs):
    terms, outs = (refs[:-2], refs[-2:])
    for kind, out in enumerate(outs):
        whole = terms[0][kind]
        for term in terms[1:]:
            whole = whole + term[kind].astype(jnp.float32)
        out[...] = whole


def sum_call(*terms):
    shape = jax.ShapeDtypeStruct(terms[0].shape[1:], jnp.float32)
    return pl.pallas_call(
        sum_kernel,
        out_shape=[shape, shape],
        in_specs=[VMEM] * len(terms),
        out_specs=[VMEM, VMEM],
        compiler_params=pltpu.CompilerParams(vmem_limit_bytes=FORWARD_LIMIT),
        cost_estimate=BACKWARD_COST,
        name="sums",
    )(*terms)


def shards(query_rows, key_rows, value_rows, out_weight, out_grad):
    heads, _, _, tokens, depth = query_rows.shape
    factor = 1.0 / math.sqrt(depth)
    scale = factor * math.log2(math.e)
    times, rows = (lax.axis_size("tm"), lax.axis_size("height"))
    both = ("tm", "height")

    def grid(pairs):
        return [(a * rows + b, a2 * rows + b2) for (a, b), (a2, b2) in pairs]

    every = [(a, b) for a in range(times) for b in range(rows)]
    crossing = [a for a in range(times) if 0 <= (a - 1 if a % 2 == 0 else a + 1) < times]

    def across(a):
        return a - 1 if a % 2 == 0 else a + 1

    up = grid([((a, b), (a, b + 1)) for a, b in every if b + 1 < rows])
    down = grid([((a, b), (a, b - 1)) for a, b in every if b >= 1])
    partner = grid([((a, b), (a ^ 1, b)) for a, b in every])
    cross = grid([((a, b), (across(a), b)) for a, b in every if a in crossing])
    cross_up = grid([((a, b), (a, b + 1)) for a, b in every if a in crossing and b + 1 < rows])
    cross_down = grid([((a, b), (a, b - 1)) for a, b in every if a in crossing and b >= 1])

    def send(value, route):
        return lax.ppermute(value, both, route)

    time, row = (lax.axis_index("tm"), lax.axis_index("height"))
    other = jnp.where(time % 2 == 0, time - 1, time + 1)
    crossed = (other >= 0) & (other < times)
    above, below = (row > 0, row < rows - 1)
    yes = row >= 0
    half = lax.axis_size("head") // 2
    side = lax.axis_index("head") // half
    valid = jnp.stack(
        [yes, above, below, yes, above, below, crossed, crossed & above, crossed & below, side > 0]
    ).astype(jnp.int32)

    queries = query_rows[:, 0, 0]
    own = jnp.stack((key_rows[:, 0, 0], value_rows[:, 0, 0]))
    out_share = out_grad.shape[0]
    grad_flat = out_grad.reshape(out_share, tokens)
    rings = [list(range(half)), list(range(half, 2 * half))]
    swap = [(i, (i + half) % (2 * half)) for i in range(2 * half)]
    swapped = lax.ppermute(grad_flat, "head", swap)
    blocks = jnp.where(
        side == 0, jnp.stack([grad_flat, swapped]), jnp.stack([swapped, grad_flat])
    ).reshape(2 * out_share, tokens)
    grad_all = lax.all_gather(blocks, "head", axis_index_groups=rings, axis=0, tiled=True)

    slabs, probs = ([None] * 9, [None] * 9)
    groups = ((0, 3), (1, 2, 6), (4, 5, 7, 8))
    order = {i: place for place, i in enumerate([i for ids in groups for i in ids])}

    def forward(ids, state):
        weight = out_weight if ids is groups[-1] else None
        got, state, extra = forward_call(
            ids, order[ids[0]], valid, queries, [slabs[i] for i in ids], state, weight, scale
        )
        for place, i in enumerate(ids):
            probs[i] = got[place]
        return (state, extra)

    slabs[0] = own
    slabs[6] = send(own, cross)
    slabs[1] = send(own, up)
    slabs[2] = send(own, down)
    slabs[3] = send(own, partner)
    state, _ = forward(groups[0], None)
    slabs[6], *state = lax.optimization_barrier((slabs[6], *state))

    slabs[7] = send(slabs[6], cross_up)
    slabs[8] = send(slabs[6], cross_down)
    slabs[4] = send(slabs[1], partner)
    slabs[5] = send(slabs[2], partner)
    state, _ = forward(groups[1], state)
    state, extra = forward(groups[2], state)
    attended, projected = extra
    levels = state[0]
    projected = lax.psum_scatter(
        projected, "head", scatter_dimension=0, axis_index_groups=rings, tiled=True
    )
    kept, given = (projected[:out_share], projected[out_share:])
    grads, weight_part = middle_call(half, times * rows, out_weight, grad_all, attended)
    weight_terms = lax.all_to_all(weight_part, both, 0, 0)

    def backward(outputs, query, added, last=False):
        return backward_call(
            outputs, order, queries, grads, attended, levels, slabs, probs, query, added, last, factor
        )

    part_7, part_8, query = backward(((7,), (8,)), None, [(), ()])
    back_up = send(part_7, cross_down)
    back_down = send(part_8, cross_up)
    part_near, part_3, query = backward(((4, 5), (3,)), query, [(), (), ()])
    weight_terms, back_up, back_down, part_near, part_3, query = lax.optimization_barrier(
        (weight_terms, back_up, back_down, part_near, part_3, query)
    )
    near = send(part_near, partner)
    near_own = send(part_3, partner)
    weight_grad = jnp.sum(weight_terms.astype(jnp.float32), axis=0).T
    kept, given, weight_grad, query = lax.optimization_barrier((kept, given, weight_grad, query))
    got = lax.ppermute(given, "head", swap)
    projected = (kept.astype(jnp.float32) + got.astype(jnp.float32)).astype(jnp.bfloat16)
    projected = projected.reshape(out_share, 1, 1, tokens)
    part_6, part_1, part_2, query = backward(
        ((6,), (1,), (2,)), query, [((back_up, None), (back_down, None)), ((near, 0),), ((near, 1),)]
    )
    far = send(part_6, cross)
    to_up = send(part_1, down)
    to_down = send(part_2, up)
    part_0, query_grad = backward(((0,),), query, [((near_own, None),)], True)
    projected, part_0 = lax.optimization_barrier((projected, part_0))
    owned = sum_call(part_0, far, to_up, to_down)
    grad_shape = (heads, 1, 1, tokens, depth)
    return (
        projected,
        query_grad.reshape(grad_shape),
        owned[0].reshape(grad_shape),
        owned[1].reshape(grad_shape),
        weight_grad,
    )


def solution(mesh):
    rows = P("head", "tm", "height", None, None)
    columns = P("head", "tm", "height", None)
    return jax.shard_map(
        shards,
        mesh=mesh,
        in_specs=(rows, rows, rows, P("head", None), columns),
        out_specs=(columns, rows, rows, rows, P("head", ("tm", "height"))),
        check_vma=False,
    )
```

```python
import functools
import math

import jax
import jax.numpy as jnp
from jax import lax
from jax.experimental import pallas as pl
from jax.experimental.pallas import tpu as pltpu
from jax.sharding import PartitionSpec as P

FORWARD_CHUNK = 256
BACKWARD_CHUNK = 256
VMEM = pl.BlockSpec(memory_space=pltpu.VMEM)
HBM = pl.BlockSpec(memory_space=pltpu.HBM)
SMEM = pl.BlockSpec(memory_space=pltpu.SMEM)
FORWARD_COST = pl.CostEstimate(flops=30 * 10**9, bytes_accessed=1000, transcendentals=0)
BACKWARD_COST = pl.CostEstimate(flops=1000000, bytes_accessed=1000, transcendentals=0)
LOWEST = -1e30
SIDE = 9
NT = (((1,), (1,)), ((), ()))
NN = (((1,), (0,)), ((), ()))
TN = (((0,), (0,)), ((), ()))
FORWARD_LIMIT = 24 * 1024 * 1024
BACKWARD_LIMIT = 34 * 1024 * 1024


def mm(a, b, dims=NN):
    return lax.dot_general(a, b, dims, preferred_element_type=jnp.float32)


def forward_kernel(ids, seen, last, scale, *refs):
    count = len(ids)
    valid, queries = refs[:2]
    pairs = refs[2 : 2 + count]
    rest = refs[2 + count :]
    if seen:
        levels_in, max_in, sum_in, acc_in = rest[:4]
        rest = rest[4:]
    if last:
        weight, rest = (rest[0], rest[1:])
    prob_out = rest[:count]
    levels, max_now, sum_now, acc_now = rest[count : count + 4]
    rest = rest[count + 4 :]
    if last:
        attended, projected, rest = (rest[0], rest[1], rest[2:])
    scores, probs, sems = (rest[:2], rest[2], rest[3])
    heads, tokens, depth = queries.shape
    if seen:
        levels[:seen] = levels_in[...]
        max_now[...] = max_in[...]
        sum_now[...] = sum_in[...]
        acc_now[...] = acc_in[...]
    else:
        max_now[...] = jnp.full(max_now.shape, LOWEST, jnp.float32)
        sum_now[...] = jnp.zeros(sum_now.shape, jnp.float32)
        acc_now[...] = jnp.zeros(acc_now.shape, jnp.float32)
    chains = [(h, c) for h in range(heads) for c in range(0, tokens, FORWARD_CHUNK)]

    def copy_out(index):
        return pltpu.make_async_copy(probs.at[index % 2], prob_out[index], sems.at[index % 2])

    for index in range(count):
        slot = index % 2
        if index >= 2:
            copy_out(index - 2).wait()

        @pl.when(valid[ids[index]] > 0)
        def _():
            pair = pairs[index]
            ones = jnp.ones((16, tokens), jnp.bfloat16)
            values = [jnp.concatenate([pair[1, h].T, ones], axis=0) for h in range(heads)]

            def score(place):
                h, c = chains[place]
                s = mm(pair[0, h], queries[h, c : c + FORWARD_CHUNK, :], NT)
                scores[place % 2][...] = s
                return jnp.max(s, axis=0, keepdims=True) * scale

            block_max = score(0)
            for place, (h, c) in enumerate(chains):
                cols = slice(c, c + FORWARD_CHUNK)
                if place + 1 < len(chains):
                    later = score(place + 1)
                before = max_now[h, :, cols]
                now = jnp.maximum(before, block_max)
                p = jnp.exp2(scores[place % 2][...] * scale - now).astype(jnp.bfloat16)
                probs[slot, h, :, cols] = p
                part = mm(values[h], p)
                fade = jnp.exp2(before - now)
                max_now[h, :, cols] = now
                acc_now[h, :, cols] = acc_now[h, :, cols] * fade + part[:depth]
                sum_now[h, :, cols] = sum_now[h, :, cols] * fade + part[depth : depth + 1]
                block_max = later

        @pl.when(valid[ids[index]] == 0)
        def _():
            probs[slot] = jnp.zeros(probs.shape[1:], jnp.bfloat16)

        levels[seen + index] = max_now[...]
        copy_out(index).start()
    if last:
        log_two = math.log2(math.e)
        levels[seen + count] = max_now[...] + jnp.log(sum_now[...]) * log_two
        for h in range(heads):
            rows = slice(h * depth, (h + 1) * depth)
            attended[rows, :] = (acc_now[h] / sum_now[h]).astype(jnp.bfloat16)
        step = heads * depth
        half = projected.shape[0] // (2 * step)
        for place in range(2 * half):
            x = valid[SIDE] if place % 2 == 0 else 1 - valid[SIDE]
            start = pl.multiple_of((x * half + place // 2) * step, step)
            part = mm(weight[:, pl.ds(start, step)], attended[...], TN)
            projected[place * step : (place + 1) * step, :] = part.astype(jnp.bfloat16)
    for index in range(max(0, count - 2), count):
        copy_out(index).wait()


def forward_call(ids, seen, valid, queries, pairs, state, weight, scale):
    count = len(ids)
    heads, tokens, depth = queries.shape
    f32, b16 = (jnp.float32, jnp.bfloat16)
    last = weight is not None
    row = jax.ShapeDtypeStruct((heads, 1, tokens), f32)
    outs = [pltpu.HBM((heads, tokens, tokens), b16)] * count
    levels_kind = pltpu.HBM if last else jax.ShapeDtypeStruct
    outs += [levels_kind((seen + count + last, heads, 1, tokens), f32), row, row]
    outs += [jax.ShapeDtypeStruct((heads, depth, tokens), f32)]
    operands = [valid, queries, *pairs] + (list(state) if seen else [])
    if last:
        operands += [weight]
        outs += [jax.ShapeDtypeStruct((heads * depth, tokens), b16)]
        outs += [pltpu.HBM((weight.shape[1], tokens), b16)]
    results = pl.pallas_call(
        functools.partial(forward_kernel, ids, seen, last, scale),
        out_shape=outs,
        in_specs=[SMEM] + [VMEM] * (len(operands) - 1),
        out_specs=[HBM] * count + [VMEM] * (len(outs) - count),
        scratch_shapes=[
            pltpu.VMEM((tokens, FORWARD_CHUNK), f32),
            pltpu.VMEM((tokens, FORWARD_CHUNK), f32),
            pltpu.VMEM((2, heads, tokens, tokens), b16),
            pltpu.SemaphoreType.DMA((2,)),
        ],
        compiler_params=pltpu.CompilerParams(vmem_limit_bytes=FORWARD_LIMIT),
        cost_estimate=FORWARD_COST,
        name="forward" + str(count),
    )(*operands)
    return (results[:count], results[count : count + 4], results[count + 4 :])


def middle_kernel(half, weight, gathered, attended, grads, terms):
    share = gathered.shape[0] // (2 * half)
    each = share // terms.shape[1]
    total = jnp.zeros(grads.shape, jnp.float32)
    for z in range(half):
        for x in range(2):
            block = gathered[(z * 2 + x) * share : (z * 2 + x + 1) * share, :]
            at = x * half + z
            total = total + mm(weight[:, at * share : (at + 1) * share], block)
            term = mm(block, attended[...], NT).astype(jnp.bfloat16)
            for e in range(each):
                terms[at * each + e] = term[e * terms.shape[1] : (e + 1) * terms.shape[1], :]
    grads[...] = total.astype(jnp.bfloat16)


def middle_call(half, shares, weight, gathered, attended):
    b16 = jnp.bfloat16
    rows, columns = weight.shape
    return pl.pallas_call(
        functools.partial(middle_kernel, half),
        out_shape=[
            jax.ShapeDtypeStruct(attended.shape, b16),
            pltpu.HBM((shares, columns // shares, rows), b16),
        ],
        in_specs=[VMEM] * 3,
        out_specs=[VMEM] * 2,
        compiler_params=pltpu.CompilerParams(vmem_limit_bytes=FORWARD_LIMIT),
        cost_estimate=BACKWARD_COST,
        name="middle",
    )(weight, pltpu.with_memory_space_constraint(gathered, pltpu.HBM), attended)


def backward_kernel(outputs, order, adds, extras, first, last, factor, *refs):
    ids = [i for group in outputs for i in group]
    count = len(ids)
    queries, grads, attended, levels = refs[:4]
    rest = refs[4:]
    pairs, prob_in, rest = (rest[:count], rest[count : 2 * count], rest[2 * count :])
    if not first:
        query_in, rest = (rest[0], rest[1:])
    added, rest = (rest[:extras], rest[extras:])
    outs, rest = (rest[: len(outputs)], rest[len(outputs) :])
    part_out = []
    for out, group in zip(outs, outputs):
        part_out += [out] if len(group) == 1 else [out.at[place] for place in range(len(group))]
    query_out, acc, grads_0, grads_1, probs, sems = rest
    score_grads = (grads_0, grads_1)
    heads, tokens, depth = queries.shape

    def copy_in(index, h):
        return pltpu.make_async_copy(prob_in[index].at[h], probs.at[index, h], sems.at[index, h])

    for index in range(count):
        for h in range(heads):
            copy_in(index, h).start()
    if first:
        acc[...] = jnp.zeros(acc.shape, jnp.float32)
    else:
        acc[...] = query_in[...]
    chains = [
        (index, h, c)
        for index in range(count)
        for h in range(heads)
        for c in range(0, tokens, BACKWARD_CHUNK)
    ]
    loads = [(index, h) for index in range(count) for h in range(heads)]
    waits = {(0, 0): loads[:1], (0, 1): loads[1:4], (2, 0): loads[4:]}
    rows = [slice(h * depth, (h + 1) * depth) for h in range(heads)]
    dots = []
    for h in range(heads):
        product = grads[rows[h], :].astype(jnp.float32) * attended[rows[h], :].astype(jnp.float32)
        dots.append(jnp.sum(product, axis=0, keepdims=True))
    grad, dot, turned = ({}, {}, {})

    def prob_grad(index, h, c):
        if c == 0:
            keep = jnp.exp2(levels[order[ids[index]], h] - levels[levels.shape[0] - 1, h])
            grad[index, h] = (grads[rows[h], :].astype(jnp.float32) * keep).astype(jnp.bfloat16)
            dot[index, h] = dots[h] * keep
            turned[index, h] = pairs[index][0, h].T
        return mm(pairs[index][1, h], grad[index, h][:, c : c + BACKWARD_CHUNK])

    def finish(index, kind, h, value):
        for which, at in adds[index]:
            ref = added[which]
            extra = ref[kind, h] if at is None else ref[at, kind, h]
            value = value + extra.astype(jnp.float32)
        part_out[index][kind, h] = value.astype(part_out[index].dtype)

    now = prob_grad(*chains[0])
    for place, (index, h, c) in enumerate(chains):
        cols = slice(c, c + BACKWARD_CHUNK)
        if place + 1 < len(chains):
            later = prob_grad(*chains[place + 1])
        if c == 0:
            for load in waits.get((index, h), ()):
                copy_in(*load).wait()
            finish(index, 1, h, mm(probs[index, h], grad[index, h], NT))
        weights = probs[index, h, :, cols].astype(jnp.float32)
        ds = (weights * (now - dot[index, h][:, cols])).astype(jnp.bfloat16)
        held = score_grads[(index * heads + h) % len(score_grads)]
        held[:, cols] = ds
        acc[h, :, cols] += mm(turned[index, h], ds)
        if c + BACKWARD_CHUNK == tokens:
            finish(index, 0, h, mm(held[...], queries[h]) * factor)
        now = later
    if last:
        for h in range(heads):
            query_out[h] = acc[h].T * factor
    else:
        query_out[...] = acc[...]


def backward_call(outputs, order, queries, grads, attended, levels, slabs, probs, query, added, last, factor):
    ids = [i for group in outputs for i in group]
    count = len(ids)
    heads, tokens, depth = queries.shape
    f32, b16 = (jnp.float32, jnp.bfloat16)
    first = query is None
    outs = []
    for group in outputs:
        several = () if len(group) == 1 else (len(group),)
        kind = jax.ShapeDtypeStruct if last else pltpu.HBM
        outs.append(kind(several + (2, heads, tokens, depth), f32 if last else b16))
    query_shape = (heads, tokens, depth) if last else (heads, depth, tokens)
    outs += [pltpu.HBM(query_shape, f32)]

    def in_hbm(value):
        return pltpu.with_memory_space_constraint(value, pltpu.HBM)

    operands = [queries, grads, attended, in_hbm(levels)]
    operands += [slabs[i] if i in (1, 2, 6) else in_hbm(slabs[i]) for i in ids]
    specs = [VMEM] * len(operands) + [HBM] * count
    operands += [in_hbm(probs[i]) for i in ids]
    operands += [] if first else [in_hbm(query)]
    arrays = []
    adds = []
    for terms in added:
        for term, _ in terms:
            if not any(term is array for array in arrays):
                arrays.append(term)
        which = [next(k for k, array in enumerate(arrays) if term is array) for term, _ in terms]
        adds.append(tuple((k, at) for k, (_, at) in zip(which, terms)))
    operands += [in_hbm(array) for array in arrays]
    results = pl.pallas_call(
        functools.partial(backward_kernel, outputs, order, tuple(adds), len(arrays), first, last, factor),
        out_shape=outs,
        in_specs=specs + [VMEM] * (len(operands) - len(specs)),
        out_specs=[VMEM] * len(outs),
        scratch_shapes=[
            pltpu.VMEM((heads, depth, tokens), f32),
            pltpu.VMEM((tokens, tokens), b16),
            pltpu.VMEM((tokens, tokens), b16),
            pltpu.VMEM((count, heads, tokens, tokens), b16),
            pltpu.SemaphoreType.DMA((count, heads)),
        ],
        compiler_params=pltpu.CompilerParams(vmem_limit_bytes=BACKWARD_LIMIT),
        cost_estimate=BACKWARD_COST,
        name="backward" + str(count),
    )(*operands)
    return results


def sum_kernel(*refs):
    terms, outs = (refs[:-2], refs[-2:])
    for kind, out in enumerate(outs):
        whole = terms[0][kind]
        for term in terms[1:]:
            whole = whole + term[kind].astype(jnp.float32)
        out[...] = whole


def sum_call(*terms):
    shape = jax.ShapeDtypeStruct(terms[0].shape[1:], jnp.float32)
    return pl.pallas_call(
        sum_kernel,
        out_shape=[shape, shape],
        in_specs=[VMEM] * len(terms),
        out_specs=[VMEM, VMEM],
        compiler_params=pltpu.CompilerParams(vmem_limit_bytes=FORWARD_LIMIT),
        cost_estimate=BACKWARD_COST,
        name="sums",
    )(*terms)


def shards(query_rows, key_rows, value_rows, out_weight, out_grad):
    heads, _, _, tokens, depth = query_rows.shape
    factor = 1.0 / math.sqrt(depth)
    scale = factor * math.log2(math.e)
    times, rows = (lax.axis_size("tm"), lax.axis_size("height"))
    both = ("tm", "height")

    def grid(pairs):
        return [(a * rows + b, a2 * rows + b2) for (a, b), (a2, b2) in pairs]

    every = [(a, b) for a in range(times) for b in range(rows)]
    crossing = [a for a in range(times) if 0 <= (a - 1 if a % 2 == 0 else a + 1) < times]

    def across(a):
        return a - 1 if a % 2 == 0 else a + 1

    up = grid([((a, b), (a, b + 1)) for a, b in every if b + 1 < rows])
    down = grid([((a, b), (a, b - 1)) for a, b in every if b >= 1])
    partner = grid([((a, b), (a ^ 1, b)) for a, b in every])
    cross = grid([((a, b), (across(a), b)) for a, b in every if a in crossing])
    cross_up = grid([((a, b), (a, b + 1)) for a, b in every if a in crossing and b + 1 < rows])
    cross_down = grid([((a, b), (a, b - 1)) for a, b in every if a in crossing and b >= 1])

    def send(value, route):
        return lax.ppermute(value, both, route)

    time, row = (lax.axis_index("tm"), lax.axis_index("height"))
    other = jnp.where(time % 2 == 0, time - 1, time + 1)
    crossed = (other >= 0) & (other < times)
    above, below = (row > 0, row < rows - 1)
    yes = row >= 0
    half = lax.axis_size("head") // 2
    side = lax.axis_index("head") // half
    valid = jnp.stack(
        [yes, above, below, yes, above, below, crossed, crossed & above, crossed & below, side > 0]
    ).astype(jnp.int32)

    queries = query_rows[:, 0, 0]
    own = jnp.stack((key_rows[:, 0, 0], value_rows[:, 0, 0]))
    out_share = out_grad.shape[0]
    grad_flat = out_grad.reshape(out_share, tokens)
    rings = [list(range(half)), list(range(half, 2 * half))]
    swap = [(i, (i + half) % (2 * half)) for i in range(2 * half)]
    swapped = lax.ppermute(grad_flat, "head", swap)
    blocks = jnp.where(
        side == 0, jnp.stack([grad_flat, swapped]), jnp.stack([swapped, grad_flat])
    ).reshape(2 * out_share, tokens)
    grad_all = lax.all_gather(blocks, "head", axis_index_groups=rings, axis=0, tiled=True)

    slabs, probs = ([None] * 9, [None] * 9)
    groups = ((0, 3), (1, 2, 6), (4, 5, 7, 8))
    order = {i: place for place, i in enumerate([i for ids in groups for i in ids])}

    def forward(ids, state):
        weight = out_weight if ids is groups[-1] else None
        got, state, extra = forward_call(
            ids, order[ids[0]], valid, queries, [slabs[i] for i in ids], state, weight, scale
        )
        for place, i in enumerate(ids):
            probs[i] = got[place]
        return (state, extra)

    slabs[0] = own
    slabs[6] = send(own, cross)
    slabs[1] = send(own, up)
    slabs[2] = send(own, down)
    slabs[3] = send(own, partner)
    state, _ = forward(groups[0], None)
    slabs[6], *state = lax.optimization_barrier((slabs[6], *state))

    slabs[7] = send(slabs[6], cross_up)
    slabs[8] = send(slabs[6], cross_down)
    slabs[4] = send(slabs[1], partner)
    slabs[5] = send(slabs[2], partner)
    state, _ = forward(groups[1], state)
    state, extra = forward(groups[2], state)
    attended, projected = extra
    levels = state[0]
    projected = lax.psum_scatter(
        projected, "head", scatter_dimension=0, axis_index_groups=rings, tiled=True
    )
    grads, weight_part = middle_call(half, times * rows, out_weight, grad_all, attended)
    weight_terms = lax.all_to_all(weight_part, both, 0, 0)

    def backward(outputs, query, added, last=False):
        return backward_call(
            outputs, order, queries, grads, attended, levels, slabs, probs, query, added, last, factor
        )

    part_7, part_8, query = backward(((7,), (8,)), None, [(), ()])
    back_up = send(part_7, cross_down)
    back_down = send(part_8, cross_up)
    part_near, part_3, query = backward(((4, 5), (3,)), query, [(), (), ()])
    weight_terms, back_up, back_down, part_near, part_3, query = lax.optimization_barrier(
        (weight_terms, back_up, back_down, part_near, part_3, query)
    )
    near = send(part_near, partner)
    near_own = send(part_3, partner)
    weight_grad = jnp.sum(weight_terms.astype(jnp.float32), axis=0).T
    projected, weight_grad, query = lax.optimization_barrier((projected, weight_grad, query))
    kept, given = (projected[:out_share], projected[out_share:])
    got = lax.ppermute(given, "head", swap)
    projected = (kept.astype(jnp.float32) + got.astype(jnp.float32)).astype(jnp.bfloat16)
    projected = projected.reshape(out_share, 1, 1, tokens)
    part_6, part_1, part_2, query = backward(
        ((6,), (1,), (2,)), query, [((back_up, None), (back_down, None)), ((near, 0),), ((near, 1),)]
    )
    far = send(part_6, cross)
    to_up = send(part_1, down)
    to_down = send(part_2, up)
    part_0, query_grad = backward(((0,),), query, [((near_own, None),)], True)
    projected, part_0 = lax.optimization_barrier((projected, part_0))
    owned = sum_call(part_0, far, to_up, to_down)
    grad_shape = (heads, 1, 1, tokens, depth)
    return (
        projected,
        query_grad.reshape(grad_shape),
        owned[0].reshape(grad_shape),
        owned[1].reshape(grad_shape),
        weight_grad,
    )


def solution(mesh):
    rows = P("head", "tm", "height", None, None)
    columns = P("head", "tm", "height", None)
    return jax.shard_map(
        shards,
        mesh=mesh,
        in_specs=(rows, rows, rows, P("head", None), columns),
        out_specs=(columns, rows, rows, rows, P("head", ("tm", "height"))),
        check_vma=False,
    )
```
